256 devices in a mesh: dp: 32 (over x, y, core), proto: 8 (over z).
Axes of the slice: x: 4, y: 4, z: 8, core: 2. Of those that a mesh axis runs over, the one named last changes fastest.
Arguments:
- teacher_feat: bfloat16 [16384, 256], P('dp'), may hold values from -6 to 6
- student_feat: bfloat16 [16384, 256], P('dp'), may hold values from -6 to 6
- teacher_protos: bfloat16 [256, 65536], P(None, 'proto'), may hold values from -0.5 to 0.5
- student_protos: bfloat16 [256, 65536], P(None, 'proto'), may hold values from -0.375 to 0.375
Outputs:
- bottleneck_grad: float32 [16384, 256], P('dp')
- proto_grad: float32 [256, 65536], P('dp', 'proto')
The draws below stay inside these ranges and needn't reach their ends.
All inputs are finite; a program needn't handle non-finite values.
Results may differ from the reference program's by a relative error of at most 0.00065.
The reference program's roundings to bfloat16 on the way (of `teacher_unit`, `teacher_wunit`, `student_unit`, `student_wunit` and `scores_grad`) count: a program that leaves them out, or rounds other values in their place, can miss the bound.
Values may be sent and summed in bfloat16 or wider, within the bound.
A program may use at most 128 MiB of HBM per device.

```python
import jax
import jax.numpy as jnp
from jax import lax

DB = 256
K = 65536
ROWS = 512
ITERS = 3
LOSS_SCALE = 256
CROPS = 16384


def shared_directions(key):
    return jnp.clip(jax.random.normal(jax.random.fold_in(key, 77), (8, DB), jnp.float32), -4.0, 4.0)


def draw_teacher_feat(key, part):
    directions = shared_directions(key)
    key = jax.random.fold_in(key, 1)
    cluster = jnp.arange(CROPS, dtype=jnp.int32) // ROWS % 8
    centers = jnp.take(directions, cluster, axis=0)
    jitter = jnp.clip(jax.random.normal(key, (CROPS, DB), jnp.float32), -4.0, 4.0)
    amplitude = 0.46
    return jnp.clip(amplitude * centers + jitter, -6.0, 6.0).astype(jnp.bfloat16)


def draw_teacher_protos(key, part):
    directions = shared_directions(key)
    key = jax.random.fold_in(key, 2)
    first_key, second_key, jitter_key = jax.random.split(key, 3)
    cluster = jnp.minimum(jax.random.randint(first_key, (K,), 0, 8), jax.random.randint(second_key, (K,), 0, 8))
    centers = jnp.take(directions, cluster, axis=0).T
    jitter = jnp.clip(jax.random.normal(jitter_key, (DB, K), jnp.float32), -4.0, 4.0)
    amplitude = 0.46
    scaled = (amplitude * centers + jitter) * DB ** (-0.5)
    return jnp.clip(scaled, -0.5, 0.5).astype(jnp.bfloat16)


def block_scale(own_key, shape, cuts, low, high):
    def one(position, parts):
        steps = jax.random.uniform(jax.random.fold_in(jax.random.fold_in(own_key, 6), position), (parts,), jnp.float32, low / len(cuts), high / len(cuts))
        return jnp.repeat(jnp.exp(steps), shape[position] // parts).reshape((-1,) + (1,) * (len(shape) - position - 1))

    level = one(*cuts[0])
    for cut in cuts[1:]:
        level = level * one(*cut)
    return level


def centred(own_key, dims, spread, reach, cuts=(), kind=jnp.bfloat16):
    array = jax.random.normal(own_key, dims, jnp.float32) * spread
    if len(cuts) > 0:
        array = block_scale(own_key, dims, cuts, -0.22, 0.18) * array
    return jnp.clip(array, min=-reach, max=reach).astype(kind)


def setup_inputs(seed: int = 0) -> dict:
    streams_of = jax.random.split(jax.random.key(seed), 5)
    return {
        "teacher_feat": draw_teacher_feat(jax.random.fold_in(streams_of[4], 71), 0),
        "student_feat": centred(streams_of[1], (CROPS, DB), 1.0, 6.0, ((0, 32),)),
        "teacher_protos": draw_teacher_protos(jax.random.fold_in(streams_of[4], 71), 0),
        "student_protos": centred(streams_of[3], (DB, K), DB ** -0.5, 0.375, ((1, 8),)),
    }


def unit_rows(x):
    x32 = x.astype(jnp.float32)
    return x32 / jnp.sqrt(lax.optimization_barrier(jnp.sum(x32 * x32, axis=-1, keepdims=True)) + 1e-06)

def unit_columns(w):
    w32 = w.astype(jnp.float32)
    return w32 / jnp.sqrt(lax.optimization_barrier(jnp.sum(w32 * w32, axis=0, keepdims=True)) + 1e-06)

def reference(teacher_feat, student_feat, teacher_protos, student_protos):
    teacher_unit = unit_rows(teacher_feat).astype(jnp.bfloat16)
    teacher_wunit = unit_columns(teacher_protos).astype(jnp.bfloat16)
    s32 = student_feat.astype(jnp.float32)
    student_norm = jnp.sqrt(lax.optimization_barrier(jnp.sum(s32 * s32, axis=-1, keepdims=True)) + 1e-06)
    student_unit32 = s32 / student_norm
    student_unit = student_unit32.astype(jnp.bfloat16)
    student_wunit = unit_columns(student_protos).astype(jnp.bfloat16)
    expo = jnp.exp(jnp.dot(teacher_unit, teacher_wunit, preferred_element_type=jnp.float32) / 0.05)
    queue = expo
    for step in range(ITERS):
        queue = queue / lax.optimization_barrier(jnp.sum(queue, axis=0, keepdims=True)) / K
        queue = queue / lax.optimization_barrier(jnp.sum(queue, axis=1, keepdims=True)) / CROPS
    targets = queue * CROPS
    sexp = jnp.exp(jnp.dot(student_unit, student_wunit, preferred_element_type=jnp.float32) / 0.1)
    probs = sexp / lax.optimization_barrier(jnp.sum(sexp, axis=1, keepdims=True))
    scores_grad = (LOSS_SCALE / 0.1 * (probs - targets)).astype(jnp.bfloat16)
    unit_grad = jnp.dot(scores_grad, student_wunit.T, preferred_element_type=jnp.float32)
    along = lax.optimization_barrier(jnp.sum(student_unit32 * unit_grad, axis=-1, keepdims=True))
    bottleneck_grad = (unit_grad - student_unit32 * along) / student_norm
    proto_grad = jnp.dot(student_unit.T, scores_grad, preferred_element_type=jnp.float32)
    return (bottleneck_grad, proto_grad)
```

```python
import functools
import math

import jax
import jax.numpy as jnp
from jax import lax
from jax.experimental import pallas as pl
from jax.experimental.pallas import tpu as pltpu
from jax.sharding import PartitionSpec as P

F32 = jnp.float32
BF16 = jnp.bfloat16
MESH = pl.DeviceIdType.MESH
ITERS = 3
GRAD_SCALE = 256 / 0.1
TEACHER_RATE = math.log2(math.e) / 0.05
STUDENT_RATE = math.log2(math.e) / 0.1
EPS = 1e-06
NX, NY, NZ = 4, 4, 8
CHIPS = NX * NY
W = 512


def unit_rows(x):
    return x / jnp.sqrt(jnp.sum(x * x, axis=-1, keepdims=True) + EPS)


def kernel(
    crops_all,
    protos_all,
    tf_hbm,
    sf_hbm,
    tw_hbm,
    sw_hbm,
    bout,
    pout,
    tf,
    sf,
    tw,
    sw,
    expo,
    sexp,
    tunit,
    sunit,
    sturn,
    smass,
    rmass,
    rscale,
    ascale,
    bscale,
    pscale,
    colpart,
    corecol,
    colsend,
    colall,
    pvec,
    rowsend,
    rowall,
    scores,
    unit_acc,
    gsend,
    gown,
    grecv,
    hold,
    land1,
    hold2,
    land2,
    unit_in,
    bres,
    ball,
    load_sem,
    feat_sem,
    cc_send,
    cc_recv,
    ca_send,
    ca_recv,
    pv_send,
    pv_recv,
    rw_send,
    rw_recv,
    g_send,
    g_recv,
    l1_send,
    l1_recv,
    l2_send,
    l2_recv,
    u_send,
    u_recv,
    b_send,
    b_recv,
):
    rows, depth = tf.shape
    width = tw.shape[1]
    half = width // 2
    steps = width // W
    hw = W // 2
    d = lax.axis_index("dp")
    z = lax.axis_index("proto")
    core = lax.rem(d, 2)
    chip = lax.div(d, 2)
    x = lax.div(chip, NY)
    y = lax.rem(chip, NY)

    def at(px, py, pc):
        return {"dp": (px * NY + py) * 2 + pc}

    mate = at(x, y, 1 - core)
    chip_peers = []
    for k in range(1, CHIPS):
        px, py = lax.rem(x + k // NY, NX), lax.rem(y + k % NY, NY)
        chip_peers.append((px * NY + py, at(px, py, core)))
    z_peers = [lax.rem(z + k, NZ) for k in range(1, NZ)]

    loads = []
    for i, (src, dst) in enumerate(((tf_hbm, tf), (sf_hbm, sf))):
        c = pltpu.make_async_copy(src, dst, feat_sem.at[i])
        c.start()
        loads.append(c)

    def load(which, src, dst, t):
        cols = pl.ds(pl.multiple_of(t * 2 * W, 2 * W), 2 * W)
        return pltpu.make_async_copy(src.at[:, cols], dst.at[:, cols], load_sem.at[which, t])

    for t in range(steps // 2):
        load(0, tw_hbm, tw, t).start()
    for t in range(steps // 2):
        load(1, sw_hbm, sw, t).start()

    barrier = pltpu.get_barrier_semaphore()
    pl.semaphore_signal(barrier, inc=1, device_id=mate, device_id_type=MESH)
    for _, dev in chip_peers:
        pl.semaphore_signal(barrier, inc=1, device_id=dev, device_id_type=MESH)
    for pz in z_peers:
        pl.semaphore_signal(barrier, inc=1, device_id={"proto": pz}, device_id_type=MESH)

    def normalize(ref, t):
        cols = pl.ds(pl.multiple_of(t * W, W), W)
        w32 = ref[:, cols].astype(F32)
        inv = 1.0 / jnp.sqrt(jnp.sum(w32 * w32, axis=0, keepdims=True) + EPS)
        ref[:, cols] = (w32 * inv).astype(BF16)

    def teacher(t, _):
        @pl.when(lax.rem(t, 2) == 0)
        def _():
            load(0, tw_hbm, tw, lax.div(t, 2)).wait()

        normalize(tw, t)
        cols = pl.ds(pl.multiple_of(t * W, W), W)
        acc = jnp.zeros((8, W), F32)
        for rb in range(rows // 128):
            rs = slice(rb * 128, rb * 128 + 128)
            e = jnp.exp2(jnp.dot(tunit[rs, :], tw[:, cols], preferred_element_type=F32) * TEACHER_RATE)
            expo[rs, cols] = e
            acc = acc + jnp.sum(e.reshape(16, 8, W), axis=0)
        off = pl.ds(pl.multiple_of(lax.rem(t, steps // 2) * W, W), W)
        colpart[lax.div(t, steps // 2), :, off] = jnp.sum(acc, axis=0, keepdims=True)
        return 0

    def student(t, _):
        @pl.when(lax.rem(t, 2) == 0)
        def _():
            load(1, sw_hbm, sw, lax.div(t, 2)).wait()

        normalize(sw, t)
        cols = pl.ds(pl.multiple_of(t * W, W), W)
        for rb in range(rows // 128):
            rs = slice(rb * 128, rb * 128 + 128)
            e = jnp.exp2(jnp.dot(sunit[rs, :], sw[:, cols], preferred_element_type=F32) * STUDENT_RATE)
            sexp[rs, cols] = e
            acc = smass[rs, :]
            for k in range(W // 128):
                acc = acc + e[:, k * 128 : (k + 1) * 128]
            smass[rs, :] = acc
        return 0

    def row_pass():
        def block(i, _):
            rs = pl.ds(pl.multiple_of(i * 64, 64), 64)

            def part(j, acc):
                for k in range(8):
                    cs = pl.ds(pl.multiple_of(j * 1024 + k * 128, 128), 128)
                    e = expo[rs, cs].reshape(8, 8, 128)
                    acc = acc + e * pscale[:, cs][None]
                return acc

            acc = lax.fori_loop(0, width // 1024, part, jnp.zeros((8, 8, 128), F32))
            rmass[rs, :] = acc.reshape(64, 128)
            return 0

        lax.fori_loop(0, rows // 64, block, 0)

    def col_pass():
        def block(j, _):
            def part(i, accs):
                for g in range(8):
                    rs = pl.ds(pl.multiple_of(i * 64 + g * 8, 8), 8)
                    r = rscale[rs, :]
                    accs = tuple(
                        a + expo[rs, pl.ds(pl.multiple_of(j * 1024 + k * 128, 128), 128)] * r
                        for k, a in enumerate(accs)
                    )
                return accs

            accs = lax.fori_loop(0, rows // 64, part, (jnp.zeros((8, 128), F32),) * 8)
            for k in range(8):
                off = lax.rem(j, 4) * 1024 + k * 128
                colpart[lax.div(j, 4), :, pl.ds(pl.multiple_of(off, 128), 128)] = jnp.sum(
                    accs[k], axis=0, keepdims=True
                )
            return 0

        lax.fori_loop(0, width // 1024, block, 0)

    def lane_total(acc):
        return jnp.sum(acc.T, axis=0, keepdims=True)

    def down(vec):
        return jnp.broadcast_to(vec, (128, rows)).T

    def core_copy(it):
        return pltpu.make_async_remote_copy(
            colpart.at[1 - core], corecol.at[it], cc_send.at[it], cc_recv.at[it], mate, MESH
        )

    def col_copy(it, i, arriving):
        q, dev = chip_peers[i]
        q = q if arriving else chip
        return pltpu.make_async_remote_copy(
            colsend.at[it], colall.at[it, q], ca_send.at[it, i], ca_recv.at[it, q], dev, MESH
        )

    def pv_copy(it, which):
        return pltpu.make_async_remote_copy(
            pvec.at[it, which], pvec.at[it, which], pv_send.at[it], pv_recv.at[it], mate, MESH
        )

    def row_copy(it, i, arriving):
        pz = z_peers[i]
        q = pz if arriving else z
        return pltpu.make_async_remote_copy(
            rowsend.at[it], rowall.at[it, q], rw_send.at[it, i], rw_recv.at[it, q], {"proto": pz}, MESH
        )

    loads[0].wait()
    tunit[...] = unit_rows(tf[...].astype(F32)).astype(BF16)
    lax.fori_loop(0, steps, teacher, 0)
    loads[1].wait()
    su = unit_rows(sf[...].astype(F32))
    sunit[...] = su.astype(BF16)
    turned = su.T.reshape(CHIPS, 2, 8, rows)
    for c in range(2):
        sturn[c] = turned[:, c].reshape(CHIPS * 8, rows).astype(BF16)
    smass[...] = jnp.zeros_like(smass)
    pl.semaphore_wait(barrier, 1 + len(chip_peers) + len(z_peers))

    share = ((0, 4), (4, 7), (7, 11), (11, 14), (14, 16), (16, 16))
    for it in range(ITERS):
        if it > 0:
            col_pass()
        cc = core_copy(it)
        cc.start()
        cc.wait()
        mine = colpart[core] + corecol[it]
        colsend[it] = mine
        colall[it, chip] = mine
        for i in range(len(chip_peers)):
            col_copy(it, i, False).start()
        lax.fori_loop(*share[2 * it], student, 0)
        for i in range(len(chip_peers)):
            col_copy(it, i, True).wait_recv()
        total = colall[it, 0]
        for q in range(1, CHIPS):
            total = total + colall[it, q]
        pvec[it, core] = 1.0 / (protos_all * total)
        pv_copy(it, core).start()
        pv_copy(it, 1 - core).wait_recv()
        for h in range(2):
            pscale[:, h * half : (h + 1) * half] = jnp.broadcast_to(pvec[it, h], (8, half))
        row_pass()
        rowsend[it, 0] = lane_total(rmass[...])
        rowsend[it, 1] = lane_total(smass[...]) if it == ITERS - 1 else jnp.zeros((1, rows), F32)
        rowall[it, z] = rowsend[it]
        for i in range(len(z_peers)):
            row_copy(it, i, False).start()
        lax.fori_loop(*share[2 * it + 1], student, 0)
        for i in range(len(z_peers)):
            row_copy(it, i, True).wait_recv()
        mass = rowall[it, 0]
        for q in range(1, NZ):
            mass = mass + rowall[it, q]
        if it < ITERS - 1:
            rscale[...] = down(1.0 / (crops_all * mass[0]))
        else:
            bscale[...] = down(GRAD_SCALE / mass[0])
            ascale[...] = down(GRAD_SCALE / mass[1])
        for i in range(len(chip_peers)):
            col_copy(it, i, False).wait_send()
        pv_copy(it, core).wait_send()
        for i in range(len(z_peers)):
            row_copy(it, i, False).wait_send()

    unit_acc[...] = jnp.zeros_like(unit_acc)

    def g_copy(t):
        return pltpu.make_async_remote_copy(
            gsend.at[lax.rem(t, 2)], grecv.at[t], g_send.at[lax.rem(t, 2)], g_recv.at[t], mate, MESH
        )

    def near(h, k):
        i, o = (x, y) if h == 0 else (y, x)
        p = lax.rem(i + k, 4)
        return i, p, (at(p, y, core) if h == 0 else at(x, p, core))

    def l1_copy(t, h, k, arriving):
        i, p, dev = near(h, k)
        s = lax.rem(t, 4)
        return pltpu.make_async_remote_copy(
            hold.at[s, h, p],
            land1.at[t, h, p if arriving else i],
            l1_send.at[s, h, k],
            l1_recv.at[t, h, p if arriving else i],
            dev,
            MESH,
        )

    def l2_copy(t, h, k, arriving):
        i, p, dev = near(1 - h, k)
        s = lax.rem(t, 4)
        return pltpu.make_async_remote_copy(
            hold2.at[s, h, p],
            land2.at[t, h, p if arriving else i],
            l2_send.at[s, h, k],
            l2_recv.at[t, h, p if arriving else i],
            dev,
            MESH,
        )

    def compute(t):
        cols = pl.ds(pl.multiple_of(t * W, W), W)
        for rb in range(rows // 64):
            rs = slice(rb * 64, rb * 64 + 64)
            a, b = ascale[rs, :], bscale[rs, :]
            for k in range(W // 128):
                cs = pl.ds(pl.multiple_of(t * W + k * 128, 128), 128)
                tgt = (expo[rs, cs].reshape(8, 8, 128) * pscale[:, cs][None]).reshape(64, 128)
                scores[rs, k * 128 : (k + 1) * 128] = (sexp[rs, cs] * a - tgt * b).astype(BF16)

        @pl.when(t >= 2)
        def _():
            g_copy(t).wait_send()

        gsend[lax.rem(t, 2)] = jnp.dot(sturn[1 - core], scores[...], preferred_element_type=F32)
        g_copy(t).start()
        gown[lax.rem(t, 2)] = jnp.dot(sturn[core], scores[...], preferred_element_type=F32)
        unit_acc[...] += lax.dot_general(
            scores[...], sw[:, cols], (((1,), (1,)), ((), ())), preferred_element_type=F32
        )

    def first(t):
        s = lax.rem(t, 4)
        g_copy(t).wait_recv()

        @pl.when(t >= 4)
        def _():
            for h in range(2):
                for k in range(1, 4):
                    l1_copy(t, h, k, False).wait_send()

        total = (gown[lax.rem(t, 2)] + grecv[t]).reshape(NX, NY, 8, W)
        hold[s, 0] = total[..., :hw]
        for i in range(NX):
            hold[s, 1, :, i] = total[i, ..., hw:]
        for h in range(2):
            for k in range(1, 4):
                l1_copy(t, h, k, False).start()
            i = near(h, 0)[0]
            land1[t, h, i] = hold[s, h, i]

    def second(t):
        s = lax.rem(t, 4)

        @pl.when(t >= 4)
        def _():
            for h in range(2):
                for k in range(1, 4):
                    l2_copy(t, h, k, False).wait_send()

        for h in range(2):
            for k in range(1, 4):
                l1_copy(t, h, k, True).wait_recv()
            total = land1[t, h, 0] + land1[t, h, 1] + land1[t, h, 2] + land1[t, h, 3]
            hold2[s, h] = total
            for k in range(1, 4):
                l2_copy(t, h, k, False).start()
            i = near(1 - h, 0)[0]
            land2[t, h, i] = hold2[s, h, i]

    def third(t):
        for h in range(2):
            for k in range(1, 4):
                l2_copy(t, h, k, True).wait_recv()
            total = land2[t, h, 0] + land2[t, h, 1] + land2[t, h, 2] + land2[t, h, 3]
            pout[:, pl.ds(pl.multiple_of(t * W + h * hw, hw), hw)] = total

    def u_copy(i, arriving):
        pz = z_peers[i]
        return pltpu.make_async_remote_copy(
            unit_acc.at[pl.ds(pl.multiple_of(pz * 64, 64), 64)],
            unit_in.at[pz if arriving else z],
            u_send.at[i],
            u_recv.at[pz if arriving else z],
            {"proto": pz},
            MESH,
        )

    def b_copy(i, arriving):
        pz = z_peers[i]
        return pltpu.make_async_remote_copy(
            bres, ball.at[pz if arriving else z], b_send.at[i], b_recv.at[pz if arriving else z], {"proto": pz}, MESH
        )

    def step(t, _):
        @pl.when(t < steps)
        def _():
            compute(t)

        @pl.when(t == steps)
        def _():
            for i in range(NZ - 1):
                u_copy(i, False).start()

        @pl.when((t >= 1) & (t < steps + 1))
        def _():
            first(t - 1)

        @pl.when((t >= 2) & (t < steps + 2))
        def _():
            second(t - 2)

        @pl.when((t >= 3) & (t < steps + 3))
        def _():
            third(t - 3)

        return 0

    lax.fori_loop(0, steps + 3, step, 0)

    mine = pl.ds(pl.multiple_of(z * 64, 64), 64)
    unit_in[z] = unit_acc[mine, :]
    for i in range(NZ - 1):
        u_copy(i, True).wait_recv()
    grad = unit_in[0]
    for q in range(1, NZ):
        grad = grad + unit_in[q]
    s32 = sf[mine, :].astype(F32)
    norm = jnp.sqrt(jnp.sum(s32 * s32, axis=-1, keepdims=True) + EPS)
    u32 = s32 / norm
    along = jnp.sum(u32 * grad, axis=-1, keepdims=True)
    res = (grad - u32 * along) / norm
    bres[...] = res
    for i in range(NZ - 1):
        b_copy(i, False).start()
    ball[z] = res
    for i in range(NZ - 1):
        b_copy(i, True).wait_recv()
    for q in range(NZ):
        bout[q * 64 : (q + 1) * 64, :] = ball[q]

    for i in range(NZ - 1):
        u_copy(i, False).wait_send()
        b_copy(i, False).wait_send()
    for t in range(steps - 2, steps):
        g_copy(t).wait_send()
    for t in range(steps - 4, steps):
        for h in range(2):
            for k in range(1, 4):
                l1_copy(t, h, k, False).wait_send()
                l2_copy(t, h, k, False).wait_send()


def body(teacher_feat, student_feat, teacher_protos, student_protos):
    rows, depth = teacher_feat.shape
    width = teacher_protos.shape[1]
    steps = width // W
    hw = W // 2
    crops_all = float(rows * lax.axis_size("dp"))
    protos_all = float(width * lax.axis_size("proto"))
    dma = pltpu.SemaphoreType.DMA
    vm = pltpu.VMEM
    anyspec = pl.BlockSpec(memory_space=pl.ANY)
    vspec = pl.BlockSpec(memory_space=pltpu.VMEM)
    return pl.pallas_call(
        functools.partial(kernel, crops_all, protos_all),
        out_shape=(
            jax.ShapeDtypeStruct((rows, depth), F32),
            jax.ShapeDtypeStruct((8, width), F32),
        ),
        in_specs=[anyspec] * 4,
        out_specs=(vspec, vspec),
        scratch_shapes=[
            vm((rows, depth), BF16),
            vm((rows, depth), BF16),
            vm((depth, width), BF16),
            vm((depth, width), BF16),
            vm((rows, width), F32),
            vm((rows, width), F32),
            vm((rows, depth), BF16),
            vm((rows, depth), BF16),
            vm((2, depth // 2, rows), BF16),
            vm((rows, 128), F32),
            vm((rows, 128), F32),
            vm((rows, 128), F32),
            vm((rows, 128), F32),
            vm((rows, 128), F32),
            vm((8, width), F32),
            vm((2, 1, width // 2), F32),
            vm((ITERS, 1, width // 2), F32),
            vm((ITERS, 1, width // 2), F32),
            vm((ITERS, CHIPS, 1, width // 2), F32),
            vm((ITERS, 2, 1, width // 2), F32),
            vm((ITERS, 2, 1, rows), F32),
            vm((ITERS, NZ, 2, 1, rows), F32),
            vm((rows, W), BF16),
            vm((rows, depth), F32),
            vm((2, depth // 2, W), F32),
            vm((2, depth // 2, W), F32),
            vm((steps, depth // 2, W), F32),
            vm((4, 2, 4, 4, 8, hw), F32),
            vm((steps, 2, 4, 4, 8, hw), F32),
            vm((4, 2, 4, 8, hw), F32),
            vm((steps, 2, 4, 8, hw), F32),
            vm((NZ, rows // NZ, depth), F32),
            vm((rows // NZ, depth), F32),
            vm((NZ, rows // NZ, depth), F32),
            dma((2, steps // 2)),
            dma((2,)),
            dma((ITERS,)),
            dma((ITERS,)),
            dma((ITERS, CHIPS)),
            dma((ITERS, CHIPS)),
            dma((ITERS,)),
            dma((ITERS,)),
            dma((ITERS, NZ)),
            dma((ITERS, NZ)),
            dma((2,)),
            dma((steps,)),
            dma((4, 2, 4)),
            dma((steps, 2, 4)),
            dma((4, 2, 4)),
            dma((steps, 2, 4)),
            dma((NZ,)),
            dma((NZ,)),
            dma((NZ,)),
            dma((NZ,)),
        ],
        compiler_params=pltpu.CompilerParams(
            collective_id=0, has_side_effects=True, vmem_limit_bytes=60 * 1024 * 1024
        ),
        name="sinkhorn_head",
    )(teacher_feat, student_feat, teacher_protos, student_protos)


def solution(mesh):
    placed = (P("dp", None), P("dp", None), P(None, "proto"), P(None, "proto"))
    return jax.shard_map(
        body,
        mesh=mesh,
        in_specs=placed,
        out_specs=(P("dp", None), P("dp", "proto")),
        check_vma=False,
    )
```

```python
import functools
import math

import jax
import jax.numpy as jnp
from jax import lax
from jax.experimental import pallas as pl
from jax.experimental.pallas import tpu as pltpu
from jax.sharding import PartitionSpec as P

F32 = jnp.float32
BF16 = jnp.bfloat16
MESH = pl.DeviceIdType.MESH
ITERS = 3
GRAD_SCALE = 256 / 0.1
TEACHER_RATE = math.log2(math.e) / 0.05
STUDENT_RATE = math.log2(math.e) / 0.1
EPS = 1e-06
TINY = 1.2e-38
NX, NY, NZ = 4, 4, 8
CHIPS = NX * NY
W = 1024
WIDE = 2048
BLOCK = 512
FINE = 256


def encode(v, power):
    square = v * v
    fourth = square * square
    return (fourth * v if power == 5 else fourth * square * v).astype(BF16)


def decode(code, power):
    c = code.astype(F32)
    size = jnp.exp2(jnp.log2(jnp.maximum(jnp.abs(c), TINY)) * (1.0 / power))
    return jnp.where(c < 0, -size, size)


def unit_rows(x):
    return x / jnp.sqrt(jnp.sum(x * x, axis=-1, keepdims=True) + EPS)


def kernel(
    crops_all,
    protos_all,
    tf_hbm,
    sf_hbm,
    tw_hbm,
    sw_hbm,
    bout,
    pout,
    tf,
    sf,
    tw,
    swt,
    expo,
    sexp,
    tunit,
    sunit,
    sturn,
    smass,
    rmass,
    rscale,
    ascale,
    bscale,
    pscale,
    colpart,
    corecol,
    colsend,
    colall,
    pvec,
    rowsend,
    rowall,
    unit_acc,
    gsend,
    gown,
    grecv,
    swap,
    land1,
    hold2,
    kept2,
    land2,
    unit_out,
    unit_in,
    bres,
    ball,
    load_sem,
    feat_sem,
    cc_send,
    cc_recv,
    ca_send,
    ca_recv,
    pv_send,
    pv_recv,
    rw_send,
    rw_recv,
    g_send,
    g_recv,
    l1_send,
    l1_recv,
    l2_send,
    l2_recv,
    u_send,
    u_recv,
    b_send,
    b_recv,
):
    rows, depth = tf.shape
    width = tw.shape[1]
    half = width // 2
    steps = width // W
    hw = W // 2
    d = lax.axis_index("dp")
    z = lax.axis_index("proto")
    core = lax.rem(d, 2)
    chip = lax.div(d, 2)
    x = lax.div(chip, NY)
    y = lax.rem(chip, NY)

    def at(px, py, pc):
        return {"dp": (px * NY + py) * 2 + pc}

    mate = at(x, y, 1 - core)
    chip_peers = []
    for k in range(1, CHIPS):
        px, py = lax.rem(x + k // NY, NX), lax.rem(y + k % NY, NY)
        chip_peers.append((px * NY + py, at(px, py, core)))
    z_peers = [lax.rem(z + k, NZ) for k in range(1, NZ)]

    loads = []
    for i, (src, dst) in enumerate(((tf_hbm, tf), (sf_hbm, sf))):
        c = pltpu.make_async_copy(src, dst, feat_sem.at[i])
        c.start()
        loads.append(c)

    def load(which, src, t):
        cols = pl.ds(pl.multiple_of(t * W, W), W)
        return pltpu.make_async_copy(src.at[:, cols], tw.at[:, cols], load_sem.at[which, t])

    for t in range(steps):
        load(0, tw_hbm, t).start()

    barrier = pltpu.get_barrier_semaphore()
    pl.semaphore_signal(barrier, inc=1, device_id=mate, device_id_type=MESH)
    for _, dev in chip_peers:
        pl.semaphore_signal(barrier, inc=1, device_id=dev, device_id_type=MESH)
    for pz in z_peers:
        pl.semaphore_signal(barrier, inc=1, device_id={"proto": pz}, device_id_type=MESH)

    def unit_block(cols):
        w32 = tw[:, cols].astype(F32)
        inv = 1.0 / jnp.sqrt(jnp.sum(w32 * w32, axis=0, keepdims=True) + EPS)
        return (w32 * inv).astype(BF16)

    def teacher(t, _):
        for i in range(WIDE // W):
            load(0, tw_hbm, t * (WIDE // W) + i).wait()
        for o in range(0, WIDE, BLOCK):
            cols = pl.ds(pl.multiple_of(t * WIDE + o, BLOCK), BLOCK)
            e = jnp.exp2(jnp.dot(tunit[...], unit_block(cols), preferred_element_type=F32) * TEACHER_RATE)
            expo[:, cols] = e
            off = pl.ds(pl.multiple_of(lax.rem(t, 2) * WIDE + o, BLOCK), BLOCK)
            colpart[lax.div(t, 2), :, off] = jnp.sum(e, axis=0, keepdims=True)
        return 0

    def student(t, _):
        for i in range(WIDE // W):
            load(1, sw_hbm, t * (WIDE // W) + i).wait()
        acc = smass[...]
        for o in range(0, WIDE, BLOCK):
            cols = pl.ds(pl.multiple_of(t * WIDE + o, BLOCK), BLOCK)
            w = unit_block(cols)
            swt[cols, :] = w.T
            e = jnp.exp2(jnp.dot(sunit[...], w, preferred_element_type=F32) * STUDENT_RATE)
            sexp[:, cols] = e
            for k in range(BLOCK // 128):
                acc = acc + e[:, k * 128 : (k + 1) * 128]
        smass[...] = acc
        return 0

    def row_pass():
        def block(i, _):
            rs = pl.ds(pl.multiple_of(i * 128, 128), 128)
            acc = [jnp.zeros((16, 8, 128), F32)] * 2
            for k in range(width // 128):
                cs = slice(k * 128, (k + 1) * 128)
                acc[k % 2] = acc[k % 2] + expo[rs, cs].reshape(16, 8, 128) * pscale[:, cs][None]
            rmass[rs, :] = (acc[0] + acc[1]).reshape(128, 128)
            return 0

        lax.fori_loop(0, rows // 128, block, 0)

    def col_pass():
        def block(j, _):
            cs = pl.ds(pl.multiple_of(j * 1024, 1024), 1024)
            acc = [jnp.zeros((8, 1024), F32)] * 2
            for i in range(rows // 8):
                r = rscale[i * 8 : i * 8 + 8, :]
                acc[i % 2] = acc[i % 2] + expo[i * 8 : i * 8 + 8, cs] * jnp.concatenate([r] * 8, axis=1)
            off = pl.ds(pl.multiple_of(lax.rem(j, 4) * 1024, 1024), 1024)
            colpart[lax.div(j, 4), :, off] = jnp.sum(acc[0] + acc[1], axis=0, keepdims=True)
            return 0

        lax.fori_loop(0, width // 1024, block, 0)

    def lane_total(acc):
        return jnp.sum(acc.T, axis=0, keepdims=True)

    def down(vec):
        return jnp.broadcast_to(vec, (128, rows)).T

    def core_copy(it):
        return pltpu.make_async_remote_copy(
            colpart.at[1 - core], corecol.at[it], cc_send.at[it], cc_recv.at[it], mate, MESH
        )

    def col_copy(it, i, arriving):
        q, dev = chip_peers[i]
        q = q if arriving else chip
        return pltpu.make_async_remote_copy(
            colsend.at[it], colall.at[it, q], ca_send.at[it, i], ca_recv.at[it, q], dev, MESH
        )

    def pv_copy(it, which):
        return pltpu.make_async_remote_copy(
            pvec.at[it, which], pvec.at[it, which], pv_send.at[it], pv_recv.at[it], mate, MESH
        )

    def row_copy(it, i, arriving):
        pz = z_peers[i]
        q = pz if arriving else z
        return pltpu.make_async_remote_copy(
            rowsend.at[it], rowall.at[it, q], rw_send.at[it, i], rw_recv.at[it, q], {"proto": pz}, MESH
        )

    loads[0].wait()
    tunit[...] = unit_rows(tf[...].astype(F32)).astype(BF16)
    lax.fori_loop(0, width // WIDE, teacher, 0)
    for t in range(steps):
        load(1, sw_hbm, t).start()
    loads[1].wait()
    su = unit_rows(sf[...].astype(F32))
    sunit[...] = su.astype(BF16)
    turned = su.T.reshape(CHIPS, 2, 8, rows)
    for c in range(2):
        sturn[c * core + (1 - c) * (1 - core)] = turned[:, c].reshape(CHIPS * 8, rows).astype(BF16)
    smass[...] = jnp.zeros_like(smass)
    pl.semaphore_wait(barrier, 1 + len(chip_peers) + len(z_peers))

    share = ((0, 1), (1, 2), (2, 3), (3, 4), (4, 4), (4, 4))
    for it in range(ITERS):
        if it > 0:
            col_pass()
        cc = core_copy(it)
        cc.start()
        cc.wait()
        mine = colpart[core] + corecol[it]
        colsend[it] = mine
        colall[it, chip] = mine
        for i in range(len(chip_peers)):
            col_copy(it, i, False).start()
        lax.fori_loop(*share[2 * it], student, 0)
        for i in range(len(chip_peers)):
            col_copy(it, i, True).wait_recv()
        total = colall[it, 0]
        for q in range(1, CHIPS):
            total = total + colall[it, q]
        pvec[it, core] = 1.0 / (protos_all * total)
        pv_copy(it, core).start()
        pv_copy(it, 1 - core).wait_recv()
        for h in range(2):
            pscale[:, h * half : (h + 1) * half] = jnp.broadcast_to(pvec[it, h], (8, half))
        row_pass()
        rowsend[it, 0] = lane_total(rmass[...])
        rowsend[it, 1] = lane_total(smass[...]) if it == ITERS - 1 else jnp.zeros((1, rows), F32)
        rowall[it, z] = rowsend[it]
        for i in range(len(z_peers)):
            row_copy(it, i, False).start()
        lax.fori_loop(*share[2 * it + 1], student, 0)
        for i in range(len(z_peers)):
            row_copy(it, i, True).wait_recv()
        mass = rowall[it, 0]
        for q in range(1, NZ):
            mass = mass + rowall[it, q]
        if it < ITERS - 1:
            rscale[...] = down(1.0 / (crops_all * mass[0]))
        else:
            bscale[...] = down(GRAD_SCALE / mass[0])
            ascale[...] = down(GRAD_SCALE / mass[1])
        for i in range(len(chip_peers)):
            col_copy(it, i, False).wait_send()
        pv_copy(it, core).wait_send()
        for i in range(len(z_peers)):
            row_copy(it, i, False).wait_send()

    unit_acc[...] = jnp.zeros_like(unit_acc)

    def g_copy(t):
        s = lax.rem(t, 3)
        return pltpu.make_async_remote_copy(gsend.at[s], grecv.at[t], g_send.at[s], g_recv.at[t], mate, MESH)

    def near(h, k):
        i, o = (x, y) if h == 0 else (y, x)
        p = lax.rem(i + k, 4)
        return i, p, (at(p, y, core) if h == 0 else at(x, p, core))

    def hold(t, h, p):
        return pl.ds(pl.multiple_of((h * 4 + p) * 32, 32), 32), pl.ds(pl.multiple_of(t * hw, hw), hw)

    def l1_copy(t, h, k, arriving):
        i, p, dev = near(h, k)
        q = p if arriving else i
        return pltpu.make_async_remote_copy(
            tw.at[hold(t, h, p)], land1.at[t, h, q], l1_send.at[t, h, k], l1_recv.at[t, h, q], dev, MESH
        )

    def l2_copy(t, h, k, arriving):
        i, p, dev = near(1 - h, k)
        q = p if arriving else i
        return pltpu.make_async_remote_copy(
            hold2.at[t, h, p], land2.at[t, h, q], l2_send.at[t, h, k], l2_recv.at[t, h, q], dev, MESH
        )

    def compute(t):
        turn = sturn[...].reshape(depth, rows)
        slot = lax.rem(t, 3)
        unit = None

        @pl.when(t >= 3)
        def _():
            g_copy(t).wait_send()

        for o in range(0, W, FINE):
            blocks = []
            for rb in range(rows // 64):
                rs = slice(rb * 64, rb * 64 + 64)
                line = []
                for k in range(FINE // 128):
                    cs = pl.ds(pl.multiple_of(t * W + o + k * 128, 128), 128)
                    tgt = (expo[rs, cs].reshape(8, 8, 128) * pscale[:, cs][None]).reshape(64, 128)
                    line.append((sexp[rs, cs] * ascale[rs, :] - tgt * bscale[rs, :]).astype(BF16))
                blocks.append(jnp.concatenate(line, axis=1))
            score = jnp.concatenate(blocks, axis=0)
            g = jnp.dot(turn, score, preferred_element_type=F32)
            gsend[slot, :, o : o + FINE] = g[: depth // 2]
            gown[slot, :, o : o + FINE] = g[depth // 2 :]
            cols = pl.ds(pl.multiple_of(t * W + o, FINE), FINE)
            part = jnp.dot(score, swt[cols, :], preferred_element_type=F32)
            unit = part if unit is None else unit + part
        unit_acc[...] += unit
        g_copy(t).start()

    def first(t):
        g_copy(t).wait_recv()
        for i in range(NX):
            part = (gown[lax.rem(t, 3), i * 32 : i * 32 + 32] + grecv[t, i * 32 : i * 32 + 32]).reshape(NY, 8, W)
            grecv[t, i * 32 : i * 32 + 32] = part.reshape(NY * 8, W)
            code = encode(part, 5)
            tw[hold(t, 0, i)] = code[..., :hw].reshape(NY * 8, hw)
            for j in range(NY):
                swap[i, j] = part[j, :, hw:]
        for j in range(NY):
            tw[hold(t, 1, j)] = encode(swap[:, j], 5).reshape(NX * 8, hw)
        for h in range(2):
            for k in range(1, 4):
                l1_copy(t, h, k, False).start()

    def second(t):
        for h in range(2):
            if h == 0:
                total = grecv[t, pl.ds(pl.multiple_of(x * 32, 32), 32), :hw].reshape(4, 8, hw)
            else:
                total = jnp.stack(
                    [grecv[t, pl.ds(pl.multiple_of(i * 32 + y * 8, 8), 8), hw:] for i in range(NX)], axis=0
                )
            for k in range(1, 4):
                l1_copy(t, h, k, True).wait_recv()
                total = total + decode(land1[t, h, near(h, k)[1]], 5).reshape(4, 8, hw)
            kept2[t, h] = total
            for i in range(4):
                v = total[i]
                hold2[t, h, i] = encode(jnp.concatenate([v[:, : hw // 2], v[:, hw // 2 :]], axis=0), 5)
            for k in range(1, 4):
                l2_copy(t, h, k, False).start()

    def third(t):
        for h in range(2):
            total = kept2[t, h, near(1 - h, 0)[0]]
            for k in range(1, 4):
                l2_copy(t, h, k, True).wait_recv()
                v = decode(land2[t, h, near(1 - h, k)[1]], 5)
                total = total + jnp.concatenate([v[:8], v[8:]], axis=1)
            pout[:, pl.ds(pl.multiple_of(t * W + h * hw, hw), hw)] = total

    def u_copy(i, arriving):
        pz = z_peers[i]
        return pltpu.make_async_remote_copy(
            unit_out.at[pz],
            unit_in.at[pz if arriving else z],
            u_send.at[i],
            u_recv.at[pz if arriving else z],
            {"proto": pz},
            MESH,
        )

    def b_copy(i, arriving):
        pz = z_peers[i]
        return pltpu.make_async_remote_copy(
            bres, ball.at[pz if arriving else z], b_send.at[i], b_recv.at[pz if arriving else z], {"proto": pz}, MESH
        )

    def step(t, _):
        compute(t)

        @pl.when(t >= 2)
        def _():
            first(t - 2)

        @pl.when(t >= 5)
        def _():
            second(t - 5)

        return 0

    def run(lo, hi, fn):
        def one(t, _):
            fn(t)
            return 0

        lax.fori_loop(lo, hi, one, 0)

    lax.fori_loop(0, steps, step, 0)
    unit_out[...] = encode(unit_acc[...], 7).reshape(NZ, rows // NZ, depth)
    for i in range(NZ - 1):
        u_copy(i, False).start()
    run(steps - 2, steps, first)
    run(steps - 5, steps - 2, second)
    run(0, 3, third)

    mine = pl.ds(pl.multiple_of(z * 64, 64), 64)
    grad = unit_acc[mine, :]
    for i in range(NZ - 1):
        u_copy(i, True).wait_recv()
        grad = grad + decode(unit_in[z_peers[i]], 7)
    u32 = unit_rows(sf[mine, :].astype(F32))
    bres[...] = encode(grad - u32 * jnp.sum(u32 * grad, axis=-1, keepdims=True), 7)
    for i in range(NZ - 1):
        b_copy(i, False).start()
    ball[z] = bres[...]

    run(steps - 2, steps, second)
    run(3, steps, third)

    for i in range(NZ - 1):
        b_copy(i, True).wait_recv()
    for q in range(NZ):
        rs = slice(q * 64, q * 64 + 64)
        s32 = sf[rs, :].astype(F32)
        norm = jnp.sqrt(jnp.sum(s32 * s32, axis=-1, keepdims=True) + EPS)
        bout[rs, :] = decode(ball[q], 7) / norm

    for i in range(NZ - 1):
        u_copy(i, False).wait_send()
        b_copy(i, False).wait_send()
    for t in range(steps - 3, steps):
        g_copy(t).wait_send()

    def drain(t):
        for h in range(2):
            for k in range(1, 4):
                l1_copy(t, h, k, False).wait_send()
                l2_copy(t, h, k, False).wait_send()

    run(0, steps, drain)


def body(teacher_feat, student_feat, teacher_protos, student_protos):
    rows, depth = teacher_feat.shape
    width = teacher_protos.shape[1]
    steps = width // W
    hw = W // 2
    crops_all = float(rows * lax.axis_size("dp"))
    protos_all = float(width * lax.axis_size("proto"))
    dma = pltpu.SemaphoreType.DMA
    vm = pltpu.VMEM
    anyspec = pl.BlockSpec(memory_space=pl.ANY)
    vspec = pl.BlockSpec(memory_space=pltpu.VMEM)
    return pl.pallas_call(
        functools.partial(kernel, crops_all, protos_all),
        out_shape=(
            jax.ShapeDtypeStruct((rows, depth), F32),
            jax.ShapeDtypeStruct((8, width), F32),
        ),
        in_specs=[anyspec] * 4,
        out_specs=(vspec, vspec),
        scratch_shapes=[
            vm((rows, depth), BF16),
            vm((rows, depth), BF16),
            vm((depth, width), BF16),
            vm((width, depth), BF16),
            vm((rows, width), F32),
            vm((rows, width), F32),
            vm((rows, depth), BF16),
            vm((rows, depth), BF16),
            vm((2, depth // 2, rows), BF16),
            vm((rows, 128), F32),
            vm((rows, 128), F32),
            vm((rows, 128), F32),
            vm((rows, 128), F32),
            vm((rows, 128), F32),
            vm((8, width), F32),
            vm((2, 1, width // 2), F32),
            vm((ITERS, 1, width // 2), F32),
            vm((ITERS, 1, width // 2), F32),
            vm((ITERS, CHIPS, 1, width // 2), F32),
            vm((ITERS, 2, 1, width // 2), F32),
            vm((ITERS, 2, 1, rows), F32),
            vm((ITERS, NZ, 2, 1, rows), F32),
            vm((rows, depth), F32),
            vm((3, depth // 2, W), F32),
            vm((3, depth // 2, W), F32),
            vm((steps, depth // 2, W), F32),
            vm((NX, NY, 8, hw), F32),
            vm((steps, 2, 4, 32, hw), BF16),
            vm((steps, 2, 4, 16, hw // 2), BF16),
            vm((steps, 2, 4, 8, hw), F32),
            vm((steps, 2, 4, 16, hw // 2), BF16),
            vm((NZ, rows // NZ, depth), BF16),
            vm((NZ, rows // NZ, depth), BF16),
            vm((rows // NZ, depth), BF16),
            vm((NZ, rows // NZ, depth), BF16),
            dma((2, steps)),
            dma((2,)),
            dma((ITERS,)),
            dma((ITERS,)),
            dma((ITERS, CHIPS)),
            dma((ITERS, CHIPS)),
            dma((ITERS,)),
            dma((ITERS,)),
            dma((ITERS, NZ)),
            dma((ITERS, NZ)),
            dma((3,)),
            dma((steps,)),
            dma((steps, 2, 4)),
            dma((steps, 2, 4)),
            dma((steps, 2, 4)),
            dma((steps, 2, 4)),
            dma((NZ,)),
            dma((NZ,)),
            dma((NZ,)),
            dma((NZ,)),
        ],
        compiler_params=pltpu.CompilerParams(
            collective_id=0, has_side_effects=True, vmem_limit_bytes=62 * 1024 * 1024
        ),
        name="sinkhorn_head",
    )(teacher_feat, student_feat, teacher_protos, student_protos)


def solution(mesh):
    placed = (P("dp", None), P("dp", None), P(None, "proto"), P(None, "proto"))
    return jax.shard_map(
        body,
        mesh=mesh,
        in_specs=placed,
        out_specs=(P("dp", None), P("dp", "proto")),
        check_vma=False,
    )
```

```python
import functools
import math

import jax
import jax.numpy as jnp
from jax import lax
from jax.experimental import pallas as pl
from jax.experimental.pallas import tpu as pltpu
from jax.sharding import PartitionSpec as P

F32 = jnp.float32
BF16 = jnp.bfloat16
MESH = pl.DeviceIdType.MESH
ITERS = 3
GRAD_SCALE = 256 / 0.1
TEACHER_RATE = math.log2(math.e) / 0.05
STUDENT_RATE = math.log2(math.e) / 0.1
EPS = 1e-06
TINY = 1.2e-38
NX, NY, NZ = 4, 4, 8
CHIPS = NX * NY
W = 1024
WIDE = 2048
BLOCK = 512
FINE = 256
PART = 32


def encode(v, power):
    square = v * v
    fourth = square * square
    return (fourth * v if power == 5 else fourth * square * v).astype(BF16)


def decode(code, power):
    c = code.astype(F32)
    size = jnp.exp2(jnp.log2(jnp.maximum(jnp.abs(c), TINY)) * (1.0 / power))
    return jnp.where(c < 0, -size, size)


def unit_rows(x):
    return x / jnp.sqrt(jnp.sum(x * x, axis=-1, keepdims=True) + EPS)


def kernel(
    crops_all,
    protos_all,
    tf_hbm,
    sf_hbm,
    tw_hbm,
    sw_hbm,
    bout,
    pout,
    tf,
    sf,
    tw,
    swt,
    expo,
    sexp,
    tunit,
    sunit,
    sturn,
    smass,
    rmass,
    rscale,
    ascale,
    bscale,
    pscale,
    colpart,
    corecol,
    colsend,
    colall,
    pvec,
    rowsend,
    rowall,
    unit_acc,
    gsend,
    gown,
    grecv,
    swap,
    land1,
    hold2,
    kept2,
    land2,
    unit_out,
    unit_in,
    bres,
    ball,
    load_sem,
    feat_sem,
    cc_send,
    cc_recv,
    ca_send,
    ca_recv,
    pv_send,
    pv_recv,
    rw_send,
    rw_recv,
    g_send,
    g_recv,
    l1_send,
    l1_recv,
    l2_send,
    l2_recv,
    u_send,
    u_recv,
    b_send,
    b_recv,
):
    rows, depth = tf.shape
    width = tw.shape[1]
    half = width // 2
    steps = width // W
    hw = W // 2
    d = lax.axis_index("dp")
    z = lax.axis_index("proto")
    core = lax.rem(d, 2)
    chip = lax.div(d, 2)
    x = lax.div(chip, NY)
    y = lax.rem(chip, NY)

    def at(px, py, pc):
        return {"dp": (px * NY + py) * 2 + pc}

    mate = at(x, y, 1 - core)
    chip_peers = []
    for k in range(1, CHIPS):
        px, py = lax.rem(x + k // NY, NX), lax.rem(y + k % NY, NY)
        chip_peers.append((px * NY + py, at(px, py, core)))
    z_peers = [lax.rem(z + k, NZ) for k in (4, 3, 5, 2, 6, 1, 7)]

    loads = []
    for i, (src, dst) in enumerate(((tf_hbm, tf), (sf_hbm, sf))):
        c = pltpu.make_async_copy(src, dst, feat_sem.at[i])
        c.start()
        loads.append(c)

    def place(t):
        h = t // (steps // 2)
        return (h * core + (1 - h) * (1 - core)) * (steps // 2) + t % (steps // 2)

    def load(which, src, t):
        cols = pl.ds(pl.multiple_of(t * W, W), W)
        mine = pl.ds(pl.multiple_of(place(t) * W, W), W)
        return pltpu.make_async_copy(src.at[:, mine], tw.at[:, cols], load_sem.at[which, t])

    for t in range(steps):
        load(0, tw_hbm, t).start()

    barrier = pltpu.get_barrier_semaphore()
    pl.semaphore_signal(barrier, inc=1, device_id=mate, device_id_type=MESH)
    for _, dev in chip_peers:
        pl.semaphore_signal(barrier, inc=1, device_id=dev, device_id_type=MESH)
    for pz in z_peers:
        pl.semaphore_signal(barrier, inc=1, device_id={"proto": pz}, device_id_type=MESH)

    def unit_block(cols):
        w32 = tw[:, cols].astype(F32)
        inv = 1.0 / jnp.sqrt(jnp.sum(w32 * w32, axis=0, keepdims=True) + EPS)
        return (w32 * inv).astype(BF16)

    def teacher(t, _):
        for i in range(WIDE // W):
            load(0, tw_hbm, t * (WIDE // W) + i).wait()
        for o in range(0, WIDE, BLOCK):
            cols = pl.ds(pl.multiple_of(t * WIDE + o, BLOCK), BLOCK)
            e = jnp.exp2(jnp.dot(tunit[...], unit_block(cols), preferred_element_type=F32) * TEACHER_RATE)
            expo[:, cols] = e
            off = pl.ds(pl.multiple_of(lax.rem(t, 2) * WIDE + o, BLOCK), BLOCK)
            colpart[lax.div(t, 2), :, off] = jnp.sum(e, axis=0, keepdims=True)
        return 0

    def student(t, _):
        for i in range(WIDE // W):
            load(1, sw_hbm, t * (WIDE // W) + i).wait()
        acc = smass[...]
        for o in range(0, WIDE, BLOCK):
            cols = pl.ds(pl.multiple_of(t * WIDE + o, BLOCK), BLOCK)
            w = unit_block(cols)
            swt[cols, :] = w.T
            e = jnp.exp2(jnp.dot(sunit[...], w, preferred_element_type=F32) * STUDENT_RATE)
            sexp[:, cols] = e
            for k in range(BLOCK // 128):
                acc = acc + e[:, k * 128 : (k + 1) * 128]
        smass[...] = acc
        return 0

    def row_pass(h, fresh):
        def block(i, _):
            rs = pl.ds(pl.multiple_of(i * 128, 128), 128)
            zero = jnp.zeros((16, 8, 128), F32)
            acc = [zero if fresh else rmass[rs, :].reshape(16, 8, 128), zero]
            for k in range(half // 128):
                cs = slice(h * half + k * 128, h * half + k * 128 + 128)
                acc[k % 2] = acc[k % 2] + expo[rs, cs].reshape(16, 8, 128) * pscale[:, cs][None]
            rmass[rs, :] = (acc[0] + acc[1]).reshape(128, 128)
            return 0

        lax.fori_loop(0, rows // 128, block, 0)

    def col_pass(h):
        def block(j, _):
            cs = pl.ds(pl.multiple_of(h * half + j * 1024, 1024), 1024)
            acc = [jnp.zeros((8, 1024), F32)] * 2
            for i in range(rows // 8):
                r = rscale[i * 8 : i * 8 + 8, :]
                acc[i % 2] = acc[i % 2] + expo[i * 8 : i * 8 + 8, cs] * jnp.concatenate([r] * 8, axis=1)
            off = pl.ds(pl.multiple_of(j * 1024, 1024), 1024)
            colpart[h, :, off] = jnp.sum(acc[0] + acc[1], axis=0, keepdims=True)
            return 0

        lax.fori_loop(0, half // 1024, block, 0)

    def spread(it, h):
        pscale[:, h * half : (h + 1) * half] = jnp.broadcast_to(pvec[it, h], (8, half))

    def lane_total(acc):
        return jnp.sum(acc.T, axis=0, keepdims=True)

    def down(vec):
        return jnp.broadcast_to(vec, (128, rows)).T

    def core_copy(it):
        return pltpu.make_async_remote_copy(
            colpart.at[0], corecol.at[it], cc_send.at[it], cc_recv.at[it], mate, MESH
        )

    def col_copy(it, i, arriving):
        q, dev = chip_peers[i]
        q = q if arriving else chip
        return pltpu.make_async_remote_copy(
            colsend.at[it], colall.at[it, q], ca_send.at[it, i], ca_recv.at[it, q], dev, MESH
        )

    def pv_copy(it):
        return pltpu.make_async_remote_copy(
            pvec.at[it, 1], pvec.at[it, 0], pv_send.at[it], pv_recv.at[it], mate, MESH
        )

    def row_copy(it, i, arriving):
        pz = z_peers[i]
        q = pz if arriving else z
        return pltpu.make_async_remote_copy(
            rowsend.at[it], rowall.at[it, q], rw_send.at[it, i], rw_recv.at[it, q], {"proto": pz}, MESH
        )

    loads[0].wait()
    tunit[...] = unit_rows(tf[...].astype(F32)).astype(BF16)
    lax.fori_loop(0, width // WIDE, teacher, 0)
    for t in range(steps):
        load(1, sw_hbm, t).start()
    pl.semaphore_wait(barrier, 1 + len(chip_peers) + len(z_peers))

    share = ((0, 1), (1, 2), (2, 3), (3, 4), (4, 4), (4, 4))
    for it in range(ITERS):
        if it > 0:
            col_pass(0)
        cc = core_copy(it)
        cc.start()
        if it > 0:
            col_pass(1)
        cc.wait()
        mine = colpart[1] + corecol[it]
        colsend[it] = mine
        colall[it, chip] = mine
        for i in range(len(chip_peers)):
            col_copy(it, i, False).start()
        if it == 0:
            loads[1].wait()
            su = unit_rows(sf[...].astype(F32))
            sunit[...] = su.astype(BF16)
            turned = su.T.reshape(CHIPS, 2, 8, rows)
            for c in range(2):
                sturn[c * core + (1 - c) * (1 - core)] = turned[:, c].reshape(CHIPS * 8, rows).astype(BF16)
            smass[...] = jnp.zeros_like(smass)
        lax.fori_loop(*share[2 * it], student, 0)
        for i in range(len(chip_peers)):
            col_copy(it, i, True).wait_recv()
        total = colall[it, 0]
        for q in range(1, CHIPS):
            total = total + colall[it, q]
        pvec[it, 1] = 1.0 / (protos_all * total)
        pv_copy(it).start()
        spread(it, 1)
        row_pass(1, True)
        pv_copy(it).wait_recv()
        spread(it, 0)
        row_pass(0, False)
        rowsend[it, 0] = lane_total(rmass[...])
        rowsend[it, 1] = lane_total(smass[...]) if it == ITERS - 1 else jnp.zeros((1, rows), F32)
        rowall[it, z] = rowsend[it]
        for i in range(len(z_peers)):
            row_copy(it, i, False).start()
        lax.fori_loop(*share[2 * it + 1], student, 0)
        for i in range(len(z_peers)):
            row_copy(it, i, True).wait_recv()
        mass = rowall[it, 0]
        for q in range(1, NZ):
            mass = mass + rowall[it, q]
        if it < ITERS - 1:
            rscale[...] = down(1.0 / (crops_all * mass[0]))
        else:
            bscale[...] = down(GRAD_SCALE / mass[0])
            ascale[...] = down(GRAD_SCALE / mass[1])
        for i in range(len(chip_peers)):
            col_copy(it, i, False).wait_send()
        pv_copy(it).wait_send()
        for i in range(len(z_peers)):
            row_copy(it, i, False).wait_send()

    unit_acc[...] = jnp.zeros_like(unit_acc)

    def g_copy(t):
        s = lax.rem(t, 3)
        return pltpu.make_async_remote_copy(gsend.at[s], grecv.at[t], g_send.at[s], g_recv.at[t], mate, MESH)

    def near(h, k):
        i, o = (x, y) if h == 0 else (y, x)
        p = lax.rem(i + k, 4)
        return i, p, (at(p, y, core) if h == 0 else at(x, p, core))

    def hold(t, h, p):
        return pl.ds(pl.multiple_of((h * 4 + p) * 32, 32), 32), pl.ds(pl.multiple_of(t * hw, hw), hw)

    def l1_copy(t, h, k, arriving):
        i, p, dev = near(h, k)
        q = p if arriving else i
        return pltpu.make_async_remote_copy(
            tw.at[hold(t, h, p)], land1.at[t, h, q], l1_send.at[t, h, k], l1_recv.at[t, h, q], dev, MESH
        )

    def l2_copy(t, h, k, arriving):
        i, p, dev = near(1 - h, k)
        q = p if arriving else i
        return pltpu.make_async_remote_copy(
            hold2.at[t, h, p], land2.at[t, h, q], l2_send.at[t, h, k], l2_recv.at[t, h, q], dev, MESH
        )

    def compute(t):
        turn = sturn[...].reshape(depth, rows)
        slot = lax.rem(t, 3)
        unit = None
        here = place(t)

        @pl.when(t >= 3)
        def _():
            g_copy(t).wait_send()

        for o in range(0, W, FINE):
            blocks = []
            for rb in range(rows // 64):
                rs = slice(rb * 64, rb * 64 + 64)
                line = []
                for k in range(FINE // 128):
                    cs = pl.ds(pl.multiple_of(here * W + o + k * 128, 128), 128)
                    tgt = (expo[rs, cs].reshape(8, 8, 128) * pscale[:, cs][None]).reshape(64, 128)
                    line.append((sexp[rs, cs] * ascale[rs, :] - tgt * bscale[rs, :]).astype(BF16))
                blocks.append(jnp.concatenate(line, axis=1))
            score = jnp.concatenate(blocks, axis=0)
            g = jnp.dot(turn, score, preferred_element_type=F32)
            gsend[slot, :, o : o + FINE] = g[: depth // 2]
            gown[slot, :, o : o + FINE] = g[depth // 2 :]
            cols = pl.ds(pl.multiple_of(here * W + o, FINE), FINE)
            part = jnp.dot(score, swt[cols, :], preferred_element_type=F32)
            unit = part if unit is None else unit + part
        unit_acc[...] += unit
        g_copy(t).start()

    def first(t):
        g_copy(t).wait_recv()
        for i in range(NX):
            part = (gown[lax.rem(t, 3), i * 32 : i * 32 + 32] + grecv[t, i * 32 : i * 32 + 32]).reshape(NY, 8, W)
            grecv[t, i * 32 : i * 32 + 32] = part.reshape(NY * 8, W)
            code = encode(part, 5)
            tw[hold(t, 0, i)] = code[..., :hw].reshape(NY * 8, hw)
            for j in range(NY):
                swap[i, j] = part[j, :, hw:]
        for j in range(NY):
            tw[hold(t, 1, j)] = encode(swap[:, j], 5).reshape(NX * 8, hw)
        for h in range(2):
            for k in range(1, 4):
                l1_copy(t, h, k, False).start()

    def second(t):
        for h in range(2):
            if h == 0:
                total = grecv[t, pl.ds(pl.multiple_of(x * 32, 32), 32), :hw].reshape(4, 8, hw)
            else:
                total = jnp.stack(
                    [grecv[t, pl.ds(pl.multiple_of(i * 32 + y * 8, 8), 8), hw:] for i in range(NX)], axis=0
                )
            for k in range(1, 4):
                l1_copy(t, h, k, True).wait_recv()
                total = total + decode(land1[t, h, near(h, k)[1]], 5).reshape(4, 8, hw)
            kept2[t, h] = total
            for i in range(4):
                v = total[i]
                hold2[t, h, i] = encode(jnp.concatenate([v[:, : hw // 2], v[:, hw // 2 :]], axis=0), 5)
            for k in range(1, 4):
                l2_copy(t, h, k, False).start()

    def third(t):
        for h in range(2):
            total = kept2[t, h, near(1 - h, 0)[0]]
            for k in range(1, 4):
                l2_copy(t, h, k, True).wait_recv()
                v = decode(land2[t, h, near(1 - h, k)[1]], 5)
                total = total + jnp.concatenate([v[:8], v[8:]], axis=1)
            pout[:, pl.ds(pl.multiple_of(t * W + h * hw, hw), hw)] = total

    def u_copy(i, part, arriving):
        pz = z_peers[i]
        q = pz if arriving else z
        rs = pl.ds(part * PART, PART)
        return pltpu.make_async_remote_copy(
            unit_out.at[pz, rs], unit_in.at[q, rs], u_send.at[part, i], u_recv.at[part, q], {"proto": pz}, MESH
        )

    def b_copy(i, part, arriving):
        pz = z_peers[i]
        q = pz if arriving else z
        rs = pl.ds(part * PART, PART)
        return pltpu.make_async_remote_copy(
            bres.at[rs], ball.at[q, rs], b_send.at[part, i], b_recv.at[part, q], {"proto": pz}, MESH
        )

    def project(part):
        rs = pl.ds(pl.multiple_of(z * 64 + part * PART, PART), PART)
        own = slice(part * PART, (part + 1) * PART)
        grad = unit_acc[rs, :]
        for i in range(NZ - 1):
            u_copy(i, part, True).wait_recv()
            grad = grad + decode(unit_in[z_peers[i], own], 7)
        u32 = unit_rows(sf[rs, :].astype(F32))
        bres[own] = encode(grad - u32 * jnp.sum(u32 * grad, axis=-1, keepdims=True), 7)
        for i in range(NZ - 1):
            b_copy(i, part, False).start()
        ball[z, own] = bres[own]

    def step(t, _):
        compute(t)

        @pl.when(t >= 2)
        def _():
            first(t - 2)

        return 0

    def run(lo, hi, fn):
        def one(t, _):
            fn(t)
            return 0

        lax.fori_loop(lo, hi, one, 0)

    lax.fori_loop(0, steps, step, 0)
    unit_out[...] = encode(unit_acc[...], 7).reshape(NZ, rows // NZ, depth)
    for part in range(2):
        for i in range(NZ - 1):
            u_copy(i, part, False).start()
    run(steps - 2, steps, first)
    run(0, steps - 2, second)
    project(0)
    run(steps - 2, steps - 1, second)
    project(1)
    run(steps - 1, steps, second)
    run(0, steps, third)

    for part in range(2):
        for i in range(NZ - 1):
            b_copy(i, part, True).wait_recv()
    bout[...] = ball[...].reshape(rows, depth)

    for part in range(2):
        for i in range(NZ - 1):
            u_copy(i, part, False).wait_send()
            b_copy(i, part, False).wait_send()
    for t in range(steps - 3, steps):
        g_copy(t).wait_send()

    def drain(t):
        for h in range(2):
            for k in range(1, 4):
                l1_copy(t, h, k, False).wait_send()
                l2_copy(t, h, k, False).wait_send()

    run(0, steps, drain)


def body(teacher_feat, student_feat, teacher_protos, student_protos):
    rows, depth = teacher_feat.shape
    width = teacher_protos.shape[1]
    steps = width // W
    hw = W // 2
    crops_all = float(rows * lax.axis_size("dp"))
    protos_all = float(width * lax.axis_size("proto"))
    dma = pltpu.SemaphoreType.DMA
    vm = pltpu.VMEM
    anyspec = pl.BlockSpec(memory_space=pl.ANY)
    vspec = pl.BlockSpec(memory_space=pltpu.VMEM)
    code, proto = pl.pallas_call(
        functools.partial(kernel, crops_all, protos_all),
        out_shape=(
            jax.ShapeDtypeStruct((rows, depth), BF16),
            jax.ShapeDtypeStruct((8, width), F32),
        ),
        in_specs=[anyspec] * 4,
        out_specs=(vspec, vspec),
        scratch_shapes=[
            vm((rows, depth), BF16),
            vm((rows, depth), BF16),
            vm((depth, width), BF16),
            vm((width, depth), BF16),
            vm((rows, width), F32),
            vm((rows, width), F32),
            vm((rows, depth), BF16),
            vm((rows, depth), BF16),
            vm((2, depth // 2, rows), BF16),
            vm((rows, 128), F32),
            vm((rows, 128), F32),
            vm((rows, 128), F32),
            vm((rows, 128), F32),
            vm((rows, 128), F32),
            vm((8, width), F32),
            vm((2, 1, width // 2), F32),
            vm((ITERS, 1, width // 2), F32),
            vm((ITERS, 1, width // 2), F32),
            vm((ITERS, CHIPS, 1, width // 2), F32),
            vm((ITERS, 2, 1, width // 2), F32),
            vm((ITERS, 2, 1, rows), F32),
            vm((ITERS, NZ, 2, 1, rows), F32),
            vm((rows, depth), F32),
            vm((3, depth // 2, W), F32),
            vm((3, depth // 2, W), F32),
            vm((steps, depth // 2, W), F32),
            vm((NX, NY, 8, hw), F32),
            vm((steps, 2, 4, 32, hw), BF16),
            vm((steps, 2, 4, 16, hw // 2), BF16),
            vm((steps, 2, 4, 8, hw), F32),
            vm((steps, 2, 4, 16, hw // 2), BF16),
            vm((NZ, rows // NZ, depth), BF16),
            vm((NZ, rows // NZ, depth), BF16),
            vm((rows // NZ, depth), BF16),
            vm((NZ, rows // NZ, depth), BF16),
            dma((2, steps)),
            dma((2,)),
            dma((ITERS,)),
            dma((ITERS,)),
            dma((ITERS, CHIPS)),
            dma((ITERS, CHIPS)),
            dma((ITERS,)),
            dma((ITERS,)),
            dma((ITERS, NZ)),
            dma((ITERS, NZ)),
            dma((3,)),
            dma((steps,)),
            dma((steps, 2, 4)),
            dma((steps, 2, 4)),
            dma((steps, 2, 4)),
            dma((steps, 2, 4)),
            dma((2, NZ)),
            dma((2, NZ)),
            dma((2, NZ)),
            dma((2, NZ)),
        ],
        compiler_params=pltpu.CompilerParams(
            collective_id=0, has_side_effects=True, vmem_limit_bytes=62 * 1024 * 1024
        ),
        name="sinkhorn_head",
    )(teacher_feat, student_feat, teacher_protos, student_protos)
    return pl.pallas_call(
        closing,
        out_shape=(jax.ShapeDtypeStruct((rows, depth), F32), jax.ShapeDtypeStruct((8, width), F32)),
        in_specs=[vspec] * 3,
        out_specs=(vspec, vspec),
        name="closing",
    )(code, student_feat, proto)


def closing(code, feat, proto, bout, pout):
    s32 = feat[...].astype(F32)
    norm = jnp.sqrt(jnp.sum(s32 * s32, axis=-1, keepdims=True) + EPS)
    bout[...] = decode(code[...], 7) / norm
    pout[...] = proto[...]


def solution(mesh):
    placed = (P("dp", None), P("dp", None), P(None, "proto"), P(None, "proto"))
    return jax.shard_map(
        body,
        mesh=mesh,
        in_specs=placed,
        out_specs=(P("dp", None), P("dp", "proto")),
        check_vma=False,
    )
```

```python
import functools
import math

import jax
import jax.numpy as jnp
from jax import lax
from jax.experimental import pallas as pl
from jax.experimental.pallas import tpu as pltpu
from jax.sharding import PartitionSpec as P

F32 = jnp.float32
BF16 = jnp.bfloat16
MESH = pl.DeviceIdType.MESH
ITERS = 3
GRAD_SCALE = 256 / 0.1
TEACHER_RATE = math.log2(math.e) / 0.05
STUDENT_RATE = math.log2(math.e) / 0.1
EPS = 1e-06
TINY = 1.2e-38
NX, NY, NZ = 4, 4, 8
CHIPS = NX * NY
W = 1024
WIDE = 2048
BLOCK = 512
FINE = 256
PART = 32
EARLY = 5
LAG = 2
FAR_FIRST = (10, 9, 11, 6, 14, 2, 8, 5, 7, 13, 15, 1, 3, 4, 12)


def encode(v, power):
    square = v * v
    fourth = square * square
    return (fourth * v if power == 5 else fourth * square * v).astype(BF16)


def decode(code, power):
    c = code.astype(F32)
    size = jnp.exp2(jnp.log2(jnp.maximum(jnp.abs(c), TINY)) * (1.0 / power))
    return jnp.where(c < 0, -size, size)


def unit_rows(x):
    return x / jnp.sqrt(jnp.sum(x * x, axis=-1, keepdims=True) + EPS)


def kernel(
    crops_all,
    protos_all,
    tf_hbm,
    sf_hbm,
    tw_hbm,
    sw_hbm,
    bout,
    pout,
    tf,
    sf,
    tw,
    swt,
    expo,
    sexp,
    tunit,
    sunit,
    sturn,
    smass,
    rmass,
    rscale,
    ascale,
    bscale,
    pscale,
    colpart,
    corecol,
    colsend,
    colall,
    pvec,
    rowsend,
    rowall,
    unit_acc,
    gsend,
    gown,
    grecv,
    swap,
    land1,
    hold2,
    kept2,
    land2,
    unit_out,
    unit_in,
    bres,
    ball,
    load_sem,
    feat_sem,
    cc_send,
    cc_recv,
    ca_send,
    ca_recv,
    pv_send,
    pv_recv,
    rw_send,
    rw_recv,
    g_send,
    g_recv,
    l1_send,
    l1_recv,
    l2_send,
    l2_recv,
    u_send,
    u_recv,
    b_send,
    b_recv,
):
    rows, depth = tf.shape
    width = tw.shape[1]
    half = width // 2
    steps = width // W
    hw = W // 2
    d = lax.axis_index("dp")
    z = lax.axis_index("proto")
    core = lax.rem(d, 2)
    chip = lax.div(d, 2)
    x = lax.div(chip, NY)
    y = lax.rem(chip, NY)

    def at(px, py, pc):
        return {"dp": (px * NY + py) * 2 + pc}

    mate = at(x, y, 1 - core)
    chip_peers = []
    for k in FAR_FIRST:
        px, py = lax.rem(x + k // NY, NX), lax.rem(y + k % NY, NY)
        chip_peers.append((px * NY + py, at(px, py, core)))
    z_peers = [lax.rem(z + k, NZ) for k in (4, 3, 5, 2, 6, 1, 7)]

    loads = []
    for i, (src, dst) in enumerate(((tf_hbm, tf), (sf_hbm, sf))):
        c = pltpu.make_async_copy(src, dst, feat_sem.at[i])
        c.start()
        loads.append(c)

    def place(t):
        h = t // (steps // 2)
        return (h * core + (1 - h) * (1 - core)) * (steps // 2) + t % (steps // 2)

    def load(which, src, t):
        cols = pl.ds(pl.multiple_of(t * W, W), W)
        mine = pl.ds(pl.multiple_of(place(t) * W, W), W)
        return pltpu.make_async_copy(src.at[:, mine], tw.at[:, cols], load_sem.at[which, t])

    for t in range(steps):
        load(0, tw_hbm, t).start()

    barrier = pltpu.get_barrier_semaphore()
    pl.semaphore_signal(barrier, inc=1, device_id=mate, device_id_type=MESH)
    for _, dev in chip_peers:
        pl.semaphore_signal(barrier, inc=1, device_id=dev, device_id_type=MESH)
    for pz in z_peers:
        pl.semaphore_signal(barrier, inc=1, device_id={"proto": pz}, device_id_type=MESH)

    def unit_block(cols):
        w32 = tw[:, cols].astype(F32)
        inv = 1.0 / jnp.sqrt(jnp.sum(w32 * w32, axis=0, keepdims=True) + EPS)
        return (w32 * inv).astype(BF16)

    def teacher(t, _):
        for i in range(WIDE // W):
            load(0, tw_hbm, t * (WIDE // W) + i).wait()
        for o in range(0, WIDE, BLOCK):
            cols = pl.ds(pl.multiple_of(t * WIDE + o, BLOCK), BLOCK)
            e = jnp.exp2(jnp.dot(tunit[...], unit_block(cols), preferred_element_type=F32) * TEACHER_RATE)
            expo[:, cols] = e
            off = pl.ds(pl.multiple_of(lax.rem(t, 2) * WIDE + o, BLOCK), BLOCK)
            colpart[lax.div(t, 2), :, off] = jnp.sum(e, axis=0, keepdims=True)
        return 0

    def student(t, _):
        for i in range(WIDE // W):
            load(1, sw_hbm, t * (WIDE // W) + i).wait()
        acc = smass[...]
        for o in range(0, WIDE, BLOCK):
            cols = pl.ds(pl.multiple_of(t * WIDE + o, BLOCK), BLOCK)
            w = unit_block(cols)
            swt[cols, :] = w.T
            e = jnp.exp2(jnp.dot(sunit[...], w, preferred_element_type=F32) * STUDENT_RATE)
            sexp[:, cols] = e
            for k in range(BLOCK // 128):
                acc = acc + e[:, k * 128 : (k + 1) * 128]
        smass[...] = acc
        return 0

    def row_pass(h, fresh):
        def block(i, _):
            rs = pl.ds(pl.multiple_of(i * 128, 128), 128)
            zero = jnp.zeros((16, 8, 128), F32)
            acc = [zero if fresh else rmass[rs, :].reshape(16, 8, 128), zero]
            for k in range(half // 128):
                cs = slice(h * half + k * 128, h * half + k * 128 + 128)
                acc[k % 2] = acc[k % 2] + expo[rs, cs].reshape(16, 8, 128) * pscale[:, cs][None]
            rmass[rs, :] = (acc[0] + acc[1]).reshape(128, 128)
            return 0

        lax.fori_loop(0, rows // 128, block, 0)

    def col_pass(h):
        def block(j, _):
            cs = pl.ds(pl.multiple_of(h * half + j * 1024, 1024), 1024)
            acc = [jnp.zeros((8, 1024), F32)] * 2
            for i in range(rows // 8):
                r = rscale[i * 8 : i * 8 + 8, :]
                acc[i % 2] = acc[i % 2] + expo[i * 8 : i * 8 + 8, cs] * jnp.concatenate([r] * 8, axis=1)
            off = pl.ds(pl.multiple_of(j * 1024, 1024), 1024)
            colpart[h, :, off] = jnp.sum(acc[0] + acc[1], axis=0, keepdims=True)
            return 0

        lax.fori_loop(0, half // 1024, block, 0)

    def spread(it, h):
        pscale[:, h * half : (h + 1) * half] = jnp.broadcast_to(pvec[it, h], (8, half))

    def lane_total(acc):
        return jnp.sum(acc.T, axis=0, keepdims=True)

    def down(vec):
        return jnp.broadcast_to(vec, (128, rows)).T

    def core_copy(it):
        return pltpu.make_async_remote_copy(
            colpart.at[0], corecol.at[it], cc_send.at[it], cc_recv.at[it], mate, MESH
        )

    def col_copy(it, i, arriving):
        q, dev = chip_peers[i]
        q = q if arriving else chip
        return pltpu.make_async_remote_copy(
            colsend.at[it], colall.at[it, q], ca_send.at[it, i], ca_recv.at[it, q], dev, MESH
        )

    def pv_copy(it):
        return pltpu.make_async_remote_copy(
            pvec.at[it, 1], pvec.at[it, 0], pv_send.at[it], pv_recv.at[it], mate, MESH
        )

    def row_copy(it, i, arriving):
        pz = z_peers[i]
        q = pz if arriving else z
        return pltpu.make_async_remote_copy(
            rowsend.at[it], rowall.at[it, q], rw_send.at[it, i], rw_recv.at[it, q], {"proto": pz}, MESH
        )

    loads[0].wait()
    tunit[...] = unit_rows(tf[...].astype(F32)).astype(BF16)
    lax.fori_loop(0, width // WIDE, teacher, 0)
    for t in range(steps):
        load(1, sw_hbm, t).start()
    pl.semaphore_wait(barrier, 1 + len(chip_peers) + len(z_peers))

    share = ((0, 1), (1, 2), (2, 3), (3, 4), (4, 4), (4, 4))
    for it in range(ITERS):
        if it > 0:
            col_pass(0)
        cc = core_copy(it)
        cc.start()
        if it > 0:
            col_pass(1)
        cc.wait()
        mine = colpart[1] + corecol[it]
        colsend[it] = mine
        colall[it, chip] = mine
        for i in range(len(chip_peers)):
            col_copy(it, i, False).start()
        if it == 0:
            loads[1].wait()
            su = unit_rows(sf[...].astype(F32))
            sunit[...] = su.astype(BF16)
            turned = su.T.reshape(CHIPS, 2, 8, rows)
            for c in range(2):
                sturn[c * core + (1 - c) * (1 - core)] = turned[:, c].reshape(CHIPS * 8, rows).astype(BF16)
            smass[...] = jnp.zeros_like(smass)
        lax.fori_loop(*share[2 * it], student, 0)
        for i in range(len(chip_peers)):
            col_copy(it, i, True).wait_recv()
        total = colall[it, 0]
        for q in range(1, CHIPS):
            total = total + colall[it, q]
        pvec[it, 1] = 1.0 / (protos_all * total)
        pv_copy(it).start()
        spread(it, 1)
        row_pass(1, True)
        pv_copy(it).wait_recv()
        spread(it, 0)
        row_pass(0, False)
        rowsend[it, 0] = lane_total(rmass[...])
        rowsend[it, 1] = lane_total(smass[...]) if it == ITERS - 1 else jnp.zeros((1, rows), F32)
        rowall[it, z] = rowsend[it]
        for i in range(len(z_peers)):
            row_copy(it, i, False).start()
        lax.fori_loop(*share[2 * it + 1], student, 0)
        for i in range(len(z_peers)):
            row_copy(it, i, True).wait_recv()
        mass = rowall[it, 0]
        for q in range(1, NZ):
            mass = mass + rowall[it, q]
        if it < ITERS - 1:
            rscale[...] = down(1.0 / (crops_all * mass[0]))
        else:
            bscale[...] = down(GRAD_SCALE / mass[0])
            ascale[...] = down(GRAD_SCALE / mass[1])
        for i in range(len(chip_peers)):
            col_copy(it, i, False).wait_send()
        pv_copy(it).wait_send()
        for i in range(len(z_peers)):
            row_copy(it, i, False).wait_send()

    unit_acc[...] = jnp.zeros_like(unit_acc)

    def g_copy(t):
        s = lax.rem(t, 3)
        return pltpu.make_async_remote_copy(gsend.at[s], grecv.at[t], g_send.at[s], g_recv.at[t], mate, MESH)

    def near(h, k):
        i, o = (x, y) if h == 0 else (y, x)
        p = lax.rem(i + k, 4)
        return i, p, (at(p, y, core) if h == 0 else at(x, p, core))

    def hold(t, h, p):
        return pl.ds(pl.multiple_of((h * 4 + p) * 32, 32), 32), pl.ds(pl.multiple_of(t * hw, hw), hw)

    def l1_copy(t, h, k, arriving):
        i, p, dev = near(h, k)
        q = p if arriving else i
        return pltpu.make_async_remote_copy(
            tw.at[hold(t, h, p)], land1.at[t, h, q], l1_send.at[t, h, k], l1_recv.at[t, h, q], dev, MESH
        )

    def l2_copy(t, h, k, arriving):
        i, p, dev = near(1 - h, k)
        q = p if arriving else i
        return pltpu.make_async_remote_copy(
            hold2.at[t, h, p], land2.at[t, h, q], l2_send.at[t, h, k], l2_recv.at[t, h, q], dev, MESH
        )

    def partial(t, o, score):
        slot = lax.rem(t, 3)
        g = jnp.dot(sturn[...].reshape(depth, rows), score, preferred_element_type=F32)
        gsend[slot, :, o : o + FINE] = g[: depth // 2]
        gown[slot, :, o : o + FINE] = g[depth // 2 :]

    def compute(t, early):
        unit = None
        here = place(t)
        if early:

            @pl.when(t >= 3)
            def _():
                g_copy(t).wait_send()

        for o in range(0, W, FINE):
            blocks = []
            for rb in range(rows // 64):
                rs = slice(rb * 64, rb * 64 + 64)
                line = []
                for k in range(FINE // 128):
                    cs = pl.ds(pl.multiple_of(here * W + o + k * 128, 128), 128)
                    tgt = (expo[rs, cs].reshape(8, 8, 128) * pscale[:, cs][None]).reshape(64, 128)
                    line.append((sexp[rs, cs] * ascale[rs, :] - tgt * bscale[rs, :]).astype(BF16))
                blocks.append(jnp.concatenate(line, axis=1))
            score = jnp.concatenate(blocks, axis=0)
            cols = pl.ds(pl.multiple_of(here * W + o, FINE), FINE)
            if early:
                partial(t, o, score)
            else:
                expo[:, cols] = score.astype(F32)
            part = jnp.dot(score, swt[cols, :], preferred_element_type=F32)
            unit = part if unit is None else unit + part
        unit_acc[...] += unit
        if early:
            g_copy(t).start()

    def late(t):
        g_copy(t).wait_send()
        here = place(t)
        for o in range(0, W, FINE):
            cols = pl.ds(pl.multiple_of(here * W + o, FINE), FINE)
            partial(t, o, expo[:, cols].astype(BF16))
        g_copy(t).start()

    def first(t):
        g_copy(t).wait_recv()
        for i in range(NX):
            part = (gown[lax.rem(t, 3), i * 32 : i * 32 + 32] + grecv[t, i * 32 : i * 32 + 32]).reshape(NY, 8, W)
            grecv[t, i * 32 : i * 32 + 32] = part.reshape(NY * 8, W)
            code = encode(part, 5)
            tw[hold(t, 0, i)] = code[..., :hw].reshape(NY * 8, hw)
            for j in range(NY):
                swap[i, j] = part[j, :, hw:]
        for j in range(NY):
            tw[hold(t, 1, j)] = encode(swap[:, j], 5).reshape(NX * 8, hw)
        for h in range(2):
            for k in (2, 1, 3):
                l1_copy(t, h, k, False).start()

    def second(t):
        for h in range(2):
            if h == 0:
                total = grecv[t, pl.ds(pl.multiple_of(x * 32, 32), 32), :hw].reshape(4, 8, hw)
            else:
                total = jnp.stack(
                    [grecv[t, pl.ds(pl.multiple_of(i * 32 + y * 8, 8), 8), hw:] for i in range(NX)], axis=0
                )
            for k in range(1, 4):
                l1_copy(t, h, k, True).wait_recv()
                total = total + decode(land1[t, h, near(h, k)[1]], 5).reshape(4, 8, hw)
            kept2[t, h] = total
            for i in range(4):
                v = total[i]
                hold2[t, h, i] = encode(jnp.concatenate([v[:, : hw // 2], v[:, hw // 2 :]], axis=0), 5)
            for k in (2, 1, 3):
                l2_copy(t, h, k, False).start()

    def third(t):
        for h in range(2):
            total = kept2[t, h, near(1 - h, 0)[0]]
            for k in range(1, 4):
                l2_copy(t, h, k, True).wait_recv()
                v = decode(land2[t, h, near(1 - h, k)[1]], 5)
                total = total + jnp.concatenate([v[:8], v[8:]], axis=1)
            pout[:, pl.ds(pl.multiple_of(t * W + h * hw, hw), hw)] = total

    def u_copy(i, part, arriving):
        pz = z_peers[i]
        q = pz if arriving else z
        rs = pl.ds(part * PART, PART)
        return pltpu.make_async_remote_copy(
            unit_out.at[pz, rs], unit_in.at[q, rs], u_send.at[part, i], u_recv.at[part, q], {"proto": pz}, MESH
        )

    def b_copy(i, part, arriving):
        pz = z_peers[i]
        q = pz if arriving else z
        rs = pl.ds(part * PART, PART)
        return pltpu.make_async_remote_copy(
            bres.at[rs], ball.at[q, rs], b_send.at[part, i], b_recv.at[part, q], {"proto": pz}, MESH
        )

    def project(part):
        rs = pl.ds(pl.multiple_of(z * 64 + part * PART, PART), PART)
        own = slice(part * PART, (part + 1) * PART)
        grad = unit_acc[rs, :]
        for i in range(NZ - 1):
            u_copy(i, part, True).wait_recv()
            grad = grad + decode(unit_in[z_peers[i], own], 7)
        u32 = unit_rows(sf[rs, :].astype(F32))
        bres[own] = encode(grad - u32 * jnp.sum(u32 * grad, axis=-1, keepdims=True), 7)
        for i in range(NZ - 1):
            b_copy(i, part, False).start()
        ball[z, own] = bres[own]

    def run(lo, hi, fn):
        def one(t, _):
            fn(t)
            return 0

        lax.fori_loop(lo, hi, one, 0)

    def inline(t):
        compute(t, True)

        @pl.when(t >= LAG)
        def _():
            first(t - LAG)

    def after(t):
        compute(t, False)

        @pl.when(t < EARLY + LAG)
        def _():
            first(t - LAG)

    def later(t):
        late(t)

        @pl.when(t >= EARLY + LAG)
        def _():
            first(t - LAG)

    run(0, EARLY, inline)
    run(EARLY, steps, after)
    unit_out[...] = encode(unit_acc[...], 7).reshape(NZ, rows // NZ, depth)
    for part in range(2):
        for i in range(NZ - 1):
            u_copy(i, part, False).start()
    run(EARLY, steps, later)
    run(steps - LAG, steps, first)
    run(0, 3, second)
    project(0)
    run(3, 4, second)
    project(1)
    run(4, steps, second)
    run(0, steps, third)

    for part in range(2):
        for i in range(NZ - 1):
            b_copy(i, part, True).wait_recv()
    bout[...] = ball[...].reshape(rows, depth)

    for part in range(2):
        for i in range(NZ - 1):
            u_copy(i, part, False).wait_send()
            b_copy(i, part, False).wait_send()
    for t in range(steps - 3, steps):
        g_copy(t).wait_send()

    def drain(t):
        for h in range(2):
            for k in range(1, 4):
                l1_copy(t, h, k, False).wait_send()
                l2_copy(t, h, k, False).wait_send()

    run(0, steps, drain)


def body(teacher_feat, student_feat, teacher_protos, student_protos):
    rows, depth = teacher_feat.shape
    width = teacher_protos.shape[1]
    steps = width // W
    hw = W // 2
    crops_all = float(rows * lax.axis_size("dp"))
    protos_all = float(width * lax.axis_size("proto"))
    dma = pltpu.SemaphoreType.DMA
    vm = pltpu.VMEM
    anyspec = pl.BlockSpec(memory_space=pl.ANY)
    vspec = pl.BlockSpec(memory_space=pltpu.VMEM)
    code, proto = pl.pallas_call(
        functools.partial(kernel, crops_all, protos_all),
        out_shape=(
            jax.ShapeDtypeStruct((rows, depth), BF16),
            jax.ShapeDtypeStruct((8, width), F32),
        ),
        in_specs=[anyspec] * 4,
        out_specs=(vspec, vspec),
        scratch_shapes=[
            vm((rows, depth), BF16),
            vm((rows, depth), BF16),
            vm((depth, width), BF16),
            vm((width, depth), BF16),
            vm((rows, width), F32),
            vm((rows, width), F32),
            vm((rows, depth), BF16),
            vm((rows, depth), BF16),
            vm((2, depth // 2, rows), BF16),
            vm((rows, 128), F32),
            vm((rows, 128), F32),
            vm((rows, 128), F32),
            vm((rows, 128), F32),
            vm((rows, 128), F32),
            vm((8, width), F32),
            vm((2, 1, width // 2), F32),
            vm((ITERS, 1, width // 2), F32),
            vm((ITERS, 1, width // 2), F32),
            vm((ITERS, CHIPS, 1, width // 2), F32),
            vm((ITERS, 2, 1, width // 2), F32),
            vm((ITERS, 2, 1, rows), F32),
            vm((ITERS, NZ, 2, 1, rows), F32),
            vm((rows, depth), F32),
            vm((3, depth // 2, W), F32),
            vm((3, depth // 2, W), F32),
            vm((steps, depth // 2, W), F32),
            vm((NX, NY, 8, hw), F32),
            vm((steps, 2, 4, 32, hw), BF16),
            vm((steps, 2, 4, 16, hw // 2), BF16),
            vm((steps, 2, 4, 8, hw), F32),
            vm((steps, 2, 4, 16, hw // 2), BF16),
            vm((NZ, rows // NZ, depth), BF16),
            vm((NZ, rows // NZ, depth), BF16),
            vm((rows // NZ, depth), BF16),
            vm((NZ, rows // NZ, depth), BF16),
            dma((2, steps)),
            dma((2,)),
            dma((ITERS,)),
            dma((ITERS,)),
            dma((ITERS, CHIPS)),
            dma((ITERS, CHIPS)),
            dma((ITERS,)),
            dma((ITERS,)),
            dma((ITERS, NZ)),
            dma((ITERS, NZ)),
            dma((3,)),
            dma((steps,)),
            dma((steps, 2, 4)),
            dma((steps, 2, 4)),
            dma((steps, 2, 4)),
            dma((steps, 2, 4)),
            dma((2, NZ)),
            dma((2, NZ)),
            dma((2, NZ)),
            dma((2, NZ)),
        ],
        compiler_params=pltpu.CompilerParams(
            collective_id=0, has_side_effects=True, vmem_limit_bytes=62 * 1024 * 1024
        ),
        name="sinkhorn_head",
    )(teacher_feat, student_feat, teacher_protos, student_protos)
    return pl.pallas_call(
        closing,
        out_shape=(jax.ShapeDtypeStruct((rows, depth), F32), jax.ShapeDtypeStruct((8, width), F32)),
        in_specs=[vspec] * 3,
        out_specs=(vspec, vspec),
        name="closing",
    )(code, student_feat, proto)


def closing(code, feat, proto, bout, pout):
    s32 = feat[...].astype(F32)
    norm = jnp.sqrt(jnp.sum(s32 * s32, axis=-1, keepdims=True) + EPS)
    bout[...] = decode(code[...], 7) / norm
    pout[...] = proto[...]


def solution(mesh):
    placed = (P("dp", None), P("dp", None), P(None, "proto"), P(None, "proto"))
    return jax.shard_map(
        body,
        mesh=mesh,
        in_specs=placed,
        out_specs=(P("dp", None), P("dp", "proto")),
        check_vma=False,
    )
```

```python
import functools
import math

import jax
import jax.numpy as jnp
from jax import lax
from jax.experimental import pallas as pl
from jax.experimental.pallas import tpu as pltpu
from jax.sharding import PartitionSpec as P

F32 = jnp.float32
BF16 = jnp.bfloat16
MESH = pl.DeviceIdType.MESH
ITERS = 3
GRAD_SCALE = 256 / 0.1
TEACHER_RATE = math.log2(math.e) / 0.05
STUDENT_RATE = math.log2(math.e) / 0.1
EPS = 1e-06
TINY = 1.2e-38
NX, NY, NZ = 4, 4, 8
CHIPS = NX * NY
W = 1024
WIDE = 2048
BLOCK = 512
FINE = 256
PART = 32
EARLY = 5
LAG = 2
FAR_FIRST = (10, 9, 11, 6, 14, 2, 8, 5, 7, 13, 15, 1, 3, 4, 12)


def encode(v, power):
    square = v * v
    fourth = square * square
    return (fourth * v if power == 5 else fourth * square * v).astype(BF16)


def decode(code, power):
    c = code.astype(F32)
    size = jnp.exp2(jnp.log2(jnp.maximum(jnp.abs(c), TINY)) * (1.0 / power))
    return jnp.where(c < 0, -size, size)


def unit_rows(x):
    return x / jnp.sqrt(jnp.sum(x * x, axis=-1, keepdims=True) + EPS)


def kernel(
    crops_all,
    protos_all,
    tf_hbm,
    sf_hbm,
    tw_hbm,
    sw_hbm,
    bout,
    pout,
    tf,
    sf,
    tw,
    swt,
    expo,
    sexp,
    tunit,
    sunit,
    sturn,
    smass,
    rmass,
    rscale,
    ascale,
    bscale,
    pscale,
    colpart,
    corecol,
    colsend,
    colall,
    pvec,
    rowsend,
    rowall,
    unit_acc,
    gsend,
    gown,
    grecv,
    swap,
    land1,
    hold2,
    kept2,
    land2,
    unit_out,
    unit_in,
    bres,
    ball,
    load_sem,
    feat_sem,
    cc_send,
    cc_recv,
    ca_send,
    ca_recv,
    pv_send,
    pv_recv,
    rw_send,
    rw_recv,
    g_send,
    g_recv,
    l1_send,
    l1_recv,
    l2_send,
    l2_recv,
    u_send,
    u_recv,
    b_send,
    b_recv,
):
    rows, depth = tf.shape
    width = tw.shape[1]
    half = width // 2
    steps = width // W
    hw = W // 2
    d = lax.axis_index("dp")
    z = lax.axis_index("proto")
    core = lax.rem(d, 2)
    chip = lax.div(d, 2)
    x = lax.div(chip, NY)
    y = lax.rem(chip, NY)

    def at(px, py, pc):
        return {"dp": (px * NY + py) * 2 + pc}

    mate = at(x, y, 1 - core)
    chip_peers = []
    for k in FAR_FIRST:
        px, py = lax.rem(x + k // NY, NX), lax.rem(y + k % NY, NY)
        chip_peers.append((px * NY + py, at(px, py, core)))
    z_peers = [lax.rem(z + k, NZ) for k in (4, 3, 5, 2, 6, 1, 7)]

    loads = []
    for i, (src, dst) in enumerate(((tf_hbm, tf), (sf_hbm, sf))):
        c = pltpu.make_async_copy(src, dst, feat_sem.at[i])
        c.start()
        loads.append(c)

    def place(t):
        h = t // (steps // 2)
        return (h * core + (1 - h) * (1 - core)) * (steps // 2) + t % (steps // 2)

    def load(which, src, t):
        cols = pl.ds(pl.multiple_of(t * W, W), W)
        mine = pl.ds(pl.multiple_of(place(t) * W, W), W)
        return pltpu.make_async_copy(src.at[:, mine], tw.at[:, cols], load_sem.at[which, t])

    for t in range(steps):
        load(0, tw_hbm, t).start()

    barrier = pltpu.get_barrier_semaphore()
    pl.semaphore_signal(barrier, inc=1, device_id=mate, device_id_type=MESH)
    for _, dev in chip_peers:
        pl.semaphore_signal(barrier, inc=1, device_id=dev, device_id_type=MESH)
    for pz in z_peers:
        pl.semaphore_signal(barrier, inc=1, device_id={"proto": pz}, device_id_type=MESH)

    def unit_block(cols):
        w32 = tw[:, cols].astype(F32)
        inv = 1.0 / jnp.sqrt(jnp.sum(w32 * w32, axis=0, keepdims=True) + EPS)
        return (w32 * inv).astype(BF16)

    def teacher(t, _):
        for i in range(WIDE // W):
            load(0, tw_hbm, t * (WIDE // W) + i).wait()
        for o in range(0, WIDE, BLOCK):
            cols = pl.ds(pl.multiple_of(t * WIDE + o, BLOCK), BLOCK)
            e = jnp.exp2(jnp.dot(tunit[...], unit_block(cols), preferred_element_type=F32) * TEACHER_RATE)
            expo[:, cols] = e
            off = pl.ds(pl.multiple_of(lax.rem(t, 2) * WIDE + o, BLOCK), BLOCK)
            colpart[lax.div(t, 2), :, off] = jnp.sum(e, axis=0, keepdims=True)
        return 0

    def student(t, _):
        for i in range(WIDE // W):
            load(1, sw_hbm, t * (WIDE // W) + i).wait()
        acc = smass[...]
        for o in range(0, WIDE, BLOCK):
            cols = pl.ds(pl.multiple_of(t * WIDE + o, BLOCK), BLOCK)
            w = unit_block(cols)
            swt[cols, :] = w.T
            e = jnp.exp2(jnp.dot(sunit[...], w, preferred_element_type=F32) * STUDENT_RATE)
            sexp[:, cols] = e
            for k in range(BLOCK // 128):
                acc = acc + e[:, k * 128 : (k + 1) * 128]
        smass[...] = acc
        return 0

    def row_pass(h, fresh):
        def block(i, _):
            rs = pl.ds(pl.multiple_of(i * 128, 128), 128)
            zero = jnp.zeros((16, 8, 128), F32)
            acc = [zero if fresh else rmass[rs, :].reshape(16, 8, 128), zero]
            for k in range(half // 128):
                cs = slice(h * half + k * 128, h * half + k * 128 + 128)
                acc[k % 2] = acc[k % 2] + expo[rs, cs].reshape(16, 8, 128) * pscale[:, cs][None]
            rmass[rs, :] = (acc[0] + acc[1]).reshape(128, 128)
            return 0

        lax.fori_loop(0, rows // 128, block, 0)

    def col_pass(h):
        def block(j, _):
            cs = pl.ds(pl.multiple_of(h * half + j * 1024, 1024), 1024)
            acc = [jnp.zeros((8, 1024), F32)] * 2
            for i in range(rows // 8):
                r = rscale[i * 8 : i * 8 + 8, :]
                acc[i % 2] = acc[i % 2] + expo[i * 8 : i * 8 + 8, cs] * jnp.concatenate([r] * 8, axis=1)
            off = pl.ds(pl.multiple_of(j * 1024, 1024), 1024)
            colpart[h, :, off] = jnp.sum(acc[0] + acc[1], axis=0, keepdims=True)
            return 0

        lax.fori_loop(0, half // 1024, block, 0)

    def spread(it, h):
        pscale[:, h * half : (h + 1) * half] = jnp.broadcast_to(pvec[it, h], (8, half))

    def lane_total(acc):
        return jnp.sum(acc.T, axis=0, keepdims=True)

    def down(vec):
        return jnp.broadcast_to(vec, (128, rows)).T

    def core_copy(it):
        return pltpu.make_async_remote_copy(
            colpart.at[0], corecol.at[it], cc_send.at[it], cc_recv.at[it], mate, MESH
        )

    def col_copy(it, i, arriving):
        q, dev = chip_peers[i]
        q = q if arriving else chip
        return pltpu.make_async_remote_copy(
            colsend.at[it], colall.at[it, q], ca_send.at[it, i], ca_recv.at[it, q], dev, MESH
        )

    def pv_copy(it):
        return pltpu.make_async_remote_copy(
            pvec.at[it, 1], pvec.at[it, 0], pv_send.at[it], pv_recv.at[it], mate, MESH
        )

    def row_copy(it, i, arriving):
        pz = z_peers[i]
        q = pz if arriving else z
        return pltpu.make_async_remote_copy(
            rowsend.at[it], rowall.at[it, q], rw_send.at[it, i], rw_recv.at[it, q], {"proto": pz}, MESH
        )

    loads[0].wait()
    tunit[...] = unit_rows(tf[...].astype(F32)).astype(BF16)
    lax.fori_loop(0, width // WIDE, teacher, 0)
    for t in range(steps):
        load(1, sw_hbm, t).start()
    pl.semaphore_wait(barrier, 1 + len(chip_peers) + len(z_peers))

    share = ((0, 1), (1, 2), (2, 3), (3, 4), (4, 4), (4, 4))
    for it in range(ITERS):
        if it > 0:
            col_pass(0)
        cc = core_copy(it)
        cc.start()
        if it > 0:
            col_pass(1)
        cc.wait()
        mine = colpart[1] + corecol[it]
        colsend[it] = mine
        colall[it, chip] = mine
        for i in range(len(chip_peers)):
            col_copy(it, i, False).start()
        if it == 0:
            loads[1].wait()
            su = unit_rows(sf[...].astype(F32))
            sunit[...] = su.astype(BF16)
            turned = su.T.reshape(CHIPS, 2, 8, rows)
            for c in range(2):
                sturn[c * core + (1 - c) * (1 - core)] = turned[:, c].reshape(CHIPS * 8, rows).astype(BF16)
            smass[...] = jnp.zeros_like(smass)
        lax.fori_loop(*share[2 * it], student, 0)
        for i in range(len(chip_peers)):
            col_copy(it, i, True).wait_recv()
        total = colall[it, 0]
        for q in range(1, CHIPS):
            total = total + colall[it, q]
        pvec[it, 1] = 1.0 / (protos_all * total)
        pv_copy(it).start()
        spread(it, 1)
        row_pass(1, True)
        pv_copy(it).wait_recv()
        spread(it, 0)
        row_pass(0, False)
        rowsend[it, 0] = lane_total(rmass[...])
        rowsend[it, 1] = lane_total(smass[...]) if it == ITERS - 1 else jnp.zeros((1, rows), F32)
        rowall[it, z] = rowsend[it]
        for i in range(len(z_peers)):
            row_copy(it, i, False).start()
        lax.fori_loop(*share[2 * it + 1], student, 0)
        for i in range(len(z_peers)):
            row_copy(it, i, True).wait_recv()
        mass = rowall[it, 0]
        for q in range(1, NZ):
            mass = mass + rowall[it, q]
        if it < ITERS - 1:
            rscale[...] = down(1.0 / (crops_all * mass[0]))
        else:
            bscale[...] = down(GRAD_SCALE / mass[0])
            ascale[...] = down(GRAD_SCALE / mass[1])
        for i in range(len(chip_peers)):
            col_copy(it, i, False).wait_send()
        pv_copy(it).wait_send()
        for i in range(len(z_peers)):
            row_copy(it, i, False).wait_send()

    unit_acc[...] = jnp.zeros_like(unit_acc)

    def g_copy(t):
        s = lax.rem(t, 3)
        return pltpu.make_async_remote_copy(gsend.at[s], grecv.at[t], g_send.at[s], g_recv.at[t], mate, MESH)

    def near(h, k):
        i, o = (x, y) if h == 0 else (y, x)
        p = lax.rem(i + k, 4)
        return i, p, (at(p, y, core) if h == 0 else at(x, p, core))

    def hold(t, h, p):
        return pl.ds(pl.multiple_of((h * 4 + p) * 32, 32), 32), pl.ds(pl.multiple_of(t * hw, hw), hw)

    def l1_copy(t, h, k, arriving):
        i, p, dev = near(h, k)
        q = p if arriving else i
        return pltpu.make_async_remote_copy(
            tw.at[hold(t, h, p)], land1.at[t, h, q], l1_send.at[t, h, k], l1_recv.at[t, h, q], dev, MESH
        )

    def l2_copy(t, h, k, arriving):
        i, p, dev = near(1 - h, k)
        q = p if arriving else i
        return pltpu.make_async_remote_copy(
            hold2.at[t, h, p], land2.at[t, h, q], l2_send.at[t, h, k], l2_recv.at[t, h, q], dev, MESH
        )

    def partial(t, o, score):
        slot = lax.rem(t, 3)
        g = jnp.dot(sturn[...].reshape(depth, rows), score, preferred_element_type=F32)
        gsend[slot, :, o : o + FINE] = g[: depth // 2]
        gown[slot, :, o : o + FINE] = g[depth // 2 :]

    def compute(t, early):
        unit = None
        here = place(t)
        if early:

            @pl.when(t >= 3)
            def _():
                g_copy(t).wait_send()

        for o in range(0, W, FINE):
            blocks = []
            for rb in range(rows // 64):
                rs = slice(rb * 64, rb * 64 + 64)
                line = []
                for k in range(FINE // 128):
                    cs = pl.ds(pl.multiple_of(here * W + o + k * 128, 128), 128)
                    tgt = (expo[rs, cs].reshape(8, 8, 128) * pscale[:, cs][None]).reshape(64, 128)
                    line.append((sexp[rs, cs] * ascale[rs, :] - tgt * bscale[rs, :]).astype(BF16))
                blocks.append(jnp.concatenate(line, axis=1))
            score = jnp.concatenate(blocks, axis=0)
            cols = pl.ds(pl.multiple_of(here * W + o, FINE), FINE)
            if early:
                partial(t, o, score)
            else:
                expo[:, cols] = score.astype(F32)
            part = jnp.dot(score, swt[cols, :], preferred_element_type=F32)
            unit = part if unit is None else unit + part
        unit_acc[...] += unit
        if early:
            g_copy(t).start()

    def late(t):
        g_copy(t).wait_send()
        here = place(t)
        for o in range(0, W, FINE):
            cols = pl.ds(pl.multiple_of(here * W + o, FINE), FINE)
            partial(t, o, expo[:, cols].astype(BF16))
        g_copy(t).start()

    def first(t):
        g_copy(t).wait_recv()
        for i in range(NX):
            part = (gown[lax.rem(t, 3), i * 32 : i * 32 + 32] + grecv[t, i * 32 : i * 32 + 32]).reshape(NY, 8, W)
            grecv[t, i * 32 : i * 32 + 32] = part.reshape(NY * 8, W)
            code = encode(part, 5)
            tw[hold(t, 0, i)] = code[..., :hw].reshape(NY * 8, hw)
            for j in range(NY):
                swap[i, j] = part[j, :, hw:]
        for j in range(NY):
            tw[hold(t, 1, j)] = encode(swap[:, j], 5).reshape(NX * 8, hw)
        for h in range(2):
            for k in (2, 1, 3):
                l1_copy(t, h, k, False).start()

    def second(t):
        for h in range(2):
            if h == 0:
                total = grecv[t, pl.ds(pl.multiple_of(x * 32, 32), 32), :hw].reshape(4, 8, hw)
            else:
                total = jnp.stack(
                    [grecv[t, pl.ds(pl.multiple_of(i * 32 + y * 8, 8), 8), hw:] for i in range(NX)], axis=0
                )
            for k in range(1, 4):
                l1_copy(t, h, k, True).wait_recv()
                total = total + decode(land1[t, h, near(h, k)[1]], 5).reshape(4, 8, hw)
            kept2[t, h] = total
            for i in range(4):
                v = total[i]
                hold2[t, h, i] = encode(jnp.concatenate([v[:, : hw // 2], v[:, hw // 2 :]], axis=0), 5)
            for k in (2, 1, 3):
                l2_copy(t, h, k, False).start()

    def third(t):
        for h in range(2):
            total = kept2[t, h, near(1 - h, 0)[0]]
            for k in range(1, 4):
                l2_copy(t, h, k, True).wait_recv()
                v = decode(land2[t, h, near(1 - h, k)[1]], 5)
                total = total + jnp.concatenate([v[:8], v[8:]], axis=1)
            pout[:, pl.ds(pl.multiple_of(t * W + h * hw, hw), hw)] = total

    def u_copy(i, part, arriving):
        pz = z_peers[i]
        q = pz if arriving else z
        rs = pl.ds(part * PART, PART)
        return pltpu.make_async_remote_copy(
            unit_out.at[pz, rs], unit_in.at[q, rs], u_send.at[part, i], u_recv.at[part, q], {"proto": pz}, MESH
        )

    def b_copy(i, part, arriving):
        pz = z_peers[i]
        q = pz if arriving else z
        rs = pl.ds(part * PART, PART)
        return pltpu.make_async_remote_copy(
            bres.at[rs], ball.at[q, rs], b_send.at[part, i], b_recv.at[part, q], {"proto": pz}, MESH
        )

    def project(part):
        rs = pl.ds(pl.multiple_of(z * 64 + part * PART, PART), PART)
        own = slice(part * PART, (part + 1) * PART)
        grad = unit_acc[rs, :]
        for i in range(NZ - 1):
            u_copy(i, part, True).wait_recv()
            grad = grad + decode(unit_in[z_peers[i], own], 7)
        u32 = unit_rows(sf[rs, :].astype(F32))
        bres[own] = encode(grad - u32 * jnp.sum(u32 * grad, axis=-1, keepdims=True), 7)
        for i in range(NZ - 1):
            b_copy(i, part, False).start()
        ball[z, own] = bres[own]

    def run(lo, hi, fn):
        def one(t, _):
            fn(t)
            return 0

        lax.fori_loop(lo, hi, one, 0)

    def inline(t):
        compute(t, True)

        @pl.when(t >= LAG)
        def _():
            first(t - LAG)

    def after(t):
        compute(t, False)

        @pl.when(t < EARLY + LAG)
        def _():
            first(t - LAG)

    def later(t):
        late(t)

        @pl.when(t >= EARLY + LAG)
        def _():
            first(t - LAG)

    run(0, EARLY, inline)
    run(EARLY, steps, after)
    unit_out[...] = encode(unit_acc[...], 7).reshape(NZ, rows // NZ, depth)
    for part in range(2):
        for i in range(NZ - 1):
            u_copy(i, part, False).start()
    run(EARLY, steps, later)
    run(steps - LAG, steps, first)
    run(0, 5, second)
    project(0)
    run(5, 6, second)
    project(1)
    run(6, steps, second)
    run(0, steps, third)

    for part in range(2):
        for i in range(NZ - 1):
            b_copy(i, part, True).wait_recv()
    bout[...] = ball[...].reshape(rows, depth)

    for part in range(2):
        for i in range(NZ - 1):
            u_copy(i, part, False).wait_send()
            b_copy(i, part, False).wait_send()
    for t in range(steps - 3, steps):
        g_copy(t).wait_send()

    def drain(t):
        for h in range(2):
            for k in range(1, 4):
                l1_copy(t, h, k, False).wait_send()
                l2_copy(t, h, k, False).wait_send()

    run(0, steps, drain)


def body(teacher_feat, student_feat, teacher_protos, student_protos):
    rows, depth = teacher_feat.shape
    width = teacher_protos.shape[1]
    steps = width // W
    hw = W // 2
    crops_all = float(rows * lax.axis_size("dp"))
    protos_all = float(width * lax.axis_size("proto"))
    dma = pltpu.SemaphoreType.DMA
    vm = pltpu.VMEM
    anyspec = pl.BlockSpec(memory_space=pl.ANY)
    vspec = pl.BlockSpec(memory_space=pltpu.VMEM)
    code, proto = pl.pallas_call(
        functools.partial(kernel, crops_all, protos_all),
        out_shape=(
            jax.ShapeDtypeStruct((rows, depth), BF16),
            jax.ShapeDtypeStruct((8, width), F32),
        ),
        in_specs=[anyspec] * 4,
        out_specs=(vspec, vspec),
        scratch_shapes=[
            vm((rows, depth), BF16),
            vm((rows, depth), BF16),
            vm((depth, width), BF16),
            vm((width, depth), BF16),
            vm((rows, width), F32),
            vm((rows, width), F32),
            vm((rows, depth), BF16),
            vm((rows, depth), BF16),
            vm((2, depth // 2, rows), BF16),
            vm((rows, 128), F32),
            vm((rows, 128), F32),
            vm((rows, 128), F32),
            vm((rows, 128), F32),
            vm((rows, 128), F32),
            vm((8, width), F32),
            vm((2, 1, width // 2), F32),
            vm((ITERS, 1, width // 2), F32),
            vm((ITERS, 1, width // 2), F32),
            vm((ITERS, CHIPS, 1, width // 2), F32),
            vm((ITERS, 2, 1, width // 2), F32),
            vm((ITERS, 2, 1, rows), F32),
            vm((ITERS, NZ, 2, 1, rows), F32),
            vm((rows, depth), F32),
            vm((3, depth // 2, W), F32),
            vm((3, depth // 2, W), F32),
            vm((steps, depth // 2, W), F32),
            vm((NX, NY, 8, hw), F32),
            vm((steps, 2, 4, 32, hw), BF16),
            vm((steps, 2, 4, 16, hw // 2), BF16),
            vm((steps, 2, 4, 8, hw), F32),
            vm((steps, 2, 4, 16, hw // 2), BF16),
            vm((NZ, rows // NZ, depth), BF16),
            vm((NZ, rows // NZ, depth), BF16),
            vm((rows // NZ, depth), BF16),
            vm((NZ, rows // NZ, depth), BF16),
            dma((2, steps)),
            dma((2,)),
            dma((ITERS,)),
            dma((ITERS,)),
            dma((ITERS, CHIPS)),
            dma((ITERS, CHIPS)),
            dma((ITERS,)),
            dma((ITERS,)),
            dma((ITERS, NZ)),
            dma((ITERS, NZ)),
            dma((3,)),
            dma((steps,)),
            dma((steps, 2, 4)),
            dma((steps, 2, 4)),
            dma((steps, 2, 4)),
            dma((steps, 2, 4)),
            dma((2, NZ)),
            dma((2, NZ)),
            dma((2, NZ)),
            dma((2, NZ)),
        ],
        compiler_params=pltpu.CompilerParams(
            collective_id=0, has_side_effects=True, vmem_limit_bytes=62 * 1024 * 1024
        ),
        name="sinkhorn_head",
    )(teacher_feat, student_feat, teacher_protos, student_protos)
    return pl.pallas_call(
        closing,
        out_shape=(jax.ShapeDtypeStruct((rows, depth), F32), jax.ShapeDtypeStruct((8, width), F32)),
        in_specs=[vspec] * 3,
        out_specs=(vspec, vspec),
        name="closing",
    )(code, student_feat, proto)


def closing(code, feat, proto, bout, pout):
    s32 = feat[...].astype(F32)
    norm = jnp.sqrt(jnp.sum(s32 * s32, axis=-1, keepdims=True) + EPS)
    bout[...] = decode(code[...], 7) / norm
    pout[...] = proto[...]


def solution(mesh):
    placed = (P("dp", None), P("dp", None), P(None, "proto"), P(None, "proto"))
    return jax.shard_map(
        body,
        mesh=mesh,
        in_specs=placed,
        out_specs=(P("dp", None), P("dp", "proto")),
        check_vma=False,
    )
```
